256 devices in a mesh: tm: 4 (over y), row: 4 (over x), col: 16 (over z, core).
Axes of the slice: x: 4, y: 4, z: 8, core: 2. Of those that a mesh axis runs over, the one named last changes fastest.
Arguments:
- features: bfloat16 [8, 64, 256, 192], P('tm', 'row', 'col'), may hold values from -6 to 6
- norm_gain: float32 [192], replicated, may hold values from 0.25 to 1.75
- conv_weight: bfloat16 [5184, 192], replicated, may hold values from -0.078125 to 0.078125
- out_grad: bfloat16 [8, 64, 256, 192], P('tm', 'row', 'col'), may hold values from -6 to 6
Outputs:
- input_grad: bfloat16 [8, 64, 256, 192], P('tm', ('row', 'col'))
- weight_grad: float32 [5184, 192], P(('row', 'col'), 'tm')
- gain_grad: float32 [192], replicated
The draws below stay inside these ranges and needn't reach their ends.
All inputs are finite; a program needn't handle non-finite values.
Results may differ from the reference program's by a relative error of at most 0.0029.
Values may be sent and summed in bfloat16 or wider, within the bound.
A program may use at most 64 MiB of HBM per device.

```python
import jax
import jax.numpy as jnp
from jax import lax

C = 192
FRAMES = 8
HEIGHT = 64
WIDTH = 256


def levels(own_key, dims, shards, smallest, top_value):
    def one(position, shards_of):
        heights = jax.random.uniform(jax.random.fold_in(jax.random.fold_in(own_key, 6), position), (shards_of,), jnp.float32, smallest / len(shards), top_value / len(shards))
        return jnp.repeat(jnp.exp(heights), dims[position] // shards_of).reshape((-1,) + (1,) * (len(dims) - position - 1))

    level = one(*shards[0])
    for cut in shards[1:]:
        level = level * one(*cut)
    return level


def centred(rng, shape, scale, bound, shards=(), held_as=jnp.bfloat16):
    entries = jax.random.normal(rng, shape, jnp.float32) * scale
    if len(shards) > 0:
        entries = levels(rng, shape, shards, -0.22, 0.18) * entries
    return jnp.clip(entries, min=-bound, max=bound).astype(held_as)


def setup_inputs(seed: int = 0) -> dict:
    key_list = jax.random.split(jax.random.key(seed), 5)
    return {
        "features": centred(key_list[0], (FRAMES, HEIGHT, WIDTH, C), 1.0, 6.0, ((0, 4), (1, 4), (2, 16))),
        "norm_gain": jnp.clip(1.0 + 0.15 * jax.random.normal(key_list[1], (C,), jnp.float32), 0.25, 1.75),
        "conv_weight": centred(key_list[2], (27 * C, C), (27 * C) ** -0.5, 0.078125),
        "out_grad": centred(key_list[3], (FRAMES, HEIGHT, WIDTH, C), 1.0, 6.0, ((0, 4), (1, 4), (2, 16))),
    }


def activate(features, norm_gain):
    scale = lax.rsqrt(lax.optimization_barrier(jnp.mean(features * features, axis=-1, keepdims=True)) + 1e-06)
    return jax.nn.silu(features * scale * norm_gain)

def reference(features, norm_gain, conv_weight, out_grad):
    feat32 = features.astype(jnp.float32)
    act32, act_vjp = jax.vjp(activate, feat32, norm_gain)
    act = act32.astype(jnp.bfloat16)
    act_pad = jnp.pad(act, ((2, 0), (1, 1), (1, 1), (0, 0)))
    grad_pad = jnp.pad(out_grad, ((0, 2), (1, 1), (1, 1), (0, 0)))
    grad_flat = out_grad.reshape(-1, C)
    blocks = []
    act_grad = jnp.zeros((FRAMES * HEIGHT * WIDTH, C), jnp.float32)
    for kt in range(3):
        for kh in range(3):
            for kw in range(3):
                k = kt * 9 + kh * 3 + kw
                moved = act_pad[kt:kt + FRAMES, kh:kh + HEIGHT, kw:kw + WIDTH].reshape(-1, C)
                blocks.append(lax.dot_general(moved, grad_flat, (((0,), (0,)), ((), ())), preferred_element_type=jnp.float32))
                later = grad_pad[2 - kt:2 - kt + FRAMES, 2 - kh:2 - kh + HEIGHT, 2 - kw:2 - kw + WIDTH].reshape(-1, C)
                block = conv_weight[k * C:(k + 1) * C]
                act_grad = act_grad + lax.dot_general(later, block, (((1,), (1,)), ((), ())), preferred_element_type=jnp.float32)
    weight_grad = jnp.concatenate(blocks, axis=0)
    feat_grad, gain_grad = act_vjp(act_grad.reshape(FRAMES, HEIGHT, WIDTH, C))
    input_grad = (out_grad.astype(jnp.float32) + feat_grad).astype(jnp.bfloat16)
    return (input_grad, weight_grad, gain_grad)
```

```python
import jax
import jax.numpy as jnp
from jax import lax
from jax.experimental import pallas as pl
from jax.experimental.pallas import tpu as pltpu
from jax.sharding import PartitionSpec as P

MESH = pl.DeviceIdType.MESH
AXES = ("tm", "row", "col")
SIZES = (4, 4, 16)
F32 = jnp.float32
BF16 = jnp.bfloat16
C = 192
EPS = 1e-06


def moved(tm=0, row=0, col=0):
    out = []
    for name, size, off in zip(AXES, SIZES, (tm, row, col)):
        out.append(lax.rem(lax.axis_index(name) + (off % size), size))
    return tuple(out)


REACHED = (
    [(-1, 0, 0), (-2, 0, 0), (-3, 0, 0)]
    + [(0, r, 0) for r in (1, 2, 3)]
    + [(-1, 1, 0), (-1, -1, 0), (-1, 0, 1), (-1, 0, -1)]
    + [(0, 0, d) for d in range(1, 16)]
)


def roll_w(x, forward):
    rows = x.shape[0]
    place = lax.rem(lax.broadcasted_iota(jnp.int32, x.shape, 0), 16)
    if forward:
        return jnp.where(place == 0, pltpu.roll(x, rows - 15, 0), pltpu.roll(x, 1, 0))
    return jnp.where(place == 15, pltpu.roll(x, 15, 0), pltpu.roll(x, rows - 1, 0))


def kernel(
    feat_hbm, gain_ref, w_hbm, grad_hbm,
    ig_out, wg_out, gg_out,
    f_v, gx, w_v, e_s, e_r, e32, act_t, part, s_lo, s_hi, r_lo, r_hi,
    ff, p1s, p1r, t_sum, vv, p2s, p2r, u_sum, p3s, p3r, gs, gr, ig,
    loc_sem, h_ss, h_rs, e_ss, e_rs, c_ss, c_rs, x_ss, x_rs, y_ss, y_rs, z_ss, z_rs,
    a_ss, a_rs, g_ss, g_rs,
):
    tm, row, col = (lax.axis_index(a) for a in AXES)
    core = lax.rem(col, 2)
    zed = col // 2
    peer = (tm, row, col + 1 - 2 * core)

    loads = [
        pltpu.make_async_copy(feat_hbm, f_v, loc_sem.at[0]),
        pltpu.make_async_copy(grad_hbm, gx.at[1, pl.ds(0, 2), pl.ds(1, 16)], loc_sem.at[1]),
        pltpu.make_async_copy(w_hbm, w_v, loc_sem.at[2]),
    ]
    for load in loads:
        load.start()

    barrier = pltpu.get_barrier_semaphore()
    for off in REACHED:
        pl.semaphore_signal(
            barrier, inc=1, device_id=moved(*[-o for o in off]), device_id_type=MESH
        )
    pl.semaphore_wait(barrier, len(REACHED))

    def remote(src, dst, ss, rs, where):
        return pltpu.make_async_remote_copy(
            src_ref=src, dst_ref=dst, send_sem=ss, recv_sem=rs, device_id=where, device_id_type=MESH
        )

    halo = [
        remote(grad_hbm.at[:, 15], gx.at[1, pl.ds(0, 2), 0], h_ss.at[0], h_rs.at[0], moved(row=1)),
        remote(grad_hbm.at[:, 0], gx.at[1, pl.ds(0, 2), 17], h_ss.at[1], h_rs.at[1], moved(row=-1)),
        remote(grad_hbm.at[:, 15], gx.at[1, pl.ds(2, 2), 0], h_ss.at[2], h_rs.at[2], moved(tm=-1, row=1)),
        remote(grad_hbm.at[:, 0], gx.at[1, pl.ds(2, 2), 17], h_ss.at[3], h_rs.at[3], moved(tm=-1, row=-1)),
        remote(grad_hbm, gx.at[1, pl.ds(2, 2), pl.ds(1, 16)], h_ss.at[4], h_rs.at[4], moved(tm=-1)),
    ]
    for copy in halo:
        copy.start()

    gain = gain_ref[...]
    loads[0].wait()
    feat = f_v[...].reshape(512, C).astype(F32)
    scale = lax.rsqrt(jnp.mean(feat * feat, axis=-1, keepdims=True) + EPS)
    normed = feat * scale * gain
    act = normed * jax.nn.sigmoid(normed)
    act = act.astype(BF16).astype(F32)
    wide = jnp.concatenate([act, jnp.zeros((512, 64), F32)], axis=1)
    for kw in range(3):
        turned = wide if kw == 1 else roll_w(wide, kw == 0)
        act_t[kw] = jnp.transpose(turned)[:C].astype(BF16)

    def insert_edges(dt):
        e32[...] = jnp.zeros_like(e32)
        for side, edge in ((0, 0), (1, 15)):
            keep = col != edge
            if dt == 1:
                keep = jnp.logical_and(keep, tm != 3)
            e32[side] = jnp.where(keep, e_r[side, dt].astype(F32), 0.0)
        place = lax.broadcasted_iota(jnp.int32, (16, C), 0)

        def one(n, carry):
            s = 2 * dt + n // 18
            h = lax.rem(n, 18)
            mid = gx[1, s, h].astype(F32)
            left = jnp.broadcast_to(e32[0, pl.ds(n, 1), :], (16, C))
            right = jnp.broadcast_to(e32[1, pl.ds(n, 1), :], (16, C))
            gx[2, s, h] = jnp.where(place == 15, left, mid).astype(BF16)
            gx[0, s, h] = jnp.where(place == 0, right, mid).astype(BF16)
            return carry

        lax.fori_loop(0, 36, one, 0, unroll=4)

    def zero_unless(keep, s, h):
        gx[1, s, h] = jnp.where(keep, gx[1, s, h].astype(F32), 0.0).astype(BF16)

    loads[1].wait()
    halo[0].wait_recv()
    halo[1].wait_recv()
    for s in range(2):
        zero_unless(row != 0, s, 0)
        zero_unless(row != 3, s, 17)
    own = gx[1, pl.ds(0, 2)].reshape(576, C)
    for side, place in ((0, 15), (1, 0)):
        r = lax.broadcasted_iota(jnp.int32, (48, 576), 0)
        q = lax.broadcasted_iota(jnp.int32, (48, 576), 1)
        pick = jnp.where(jnp.logical_and(q == 16 * r + place, r < 36), 1.0, 0.0).astype(BF16)
        e_s[side] = jnp.dot(pick, own, preferred_element_type=F32).astype(BF16)
    edges = []
    for dt in range(2):
        for side, step in ((0, 1), (1, -1)):
            i = 2 * dt + side
            edges.append(
                remote(e_s.at[side], e_r.at[side, dt], e_ss.at[i], e_rs.at[i], moved(tm=-dt, col=step))
            )
    for copy in edges:
        copy.start()

    def taps(kt):
        def one(j, carry):
            kh = j // 3
            kw = lax.rem(j, 3)
            k = 9 * kt + j
            cells = gx[kw, pl.ds(2 - kt, 2), pl.ds(2 - kh, 16)].reshape(512, C)
            more = lax.dot_general(
                cells, w_v[k], (((1,), (1,)), ((), ())), preferred_element_type=F32
            )
            part[kw] = part[kw] + more
            wg = jnp.dot(act_t[kw], cells, preferred_element_type=F32)
            rows = pl.ds(pl.multiple_of(192 * k, 8), 192)
            s_lo[rows, :] = wg[:, :128]
            s_hi[rows, pl.ds(0, 64)] = wg[:, 128:]
            return carry

        lax.fori_loop(0, 9, one, 0)

    def to_peer(first, count):
        def one(m, carry):
            start = pl.multiple_of((81 * (2 * m + 1 - core)) // 8 * 8, 8)
            rows = pl.ds(start, 88)
            remote(s_lo.at[rows], r_lo.at[rows], c_ss.at[0], c_rs.at[0], peer).start()
            remote(s_hi.at[rows], r_hi.at[rows], c_ss.at[1], c_rs.at[1], peer).start()
            return carry

        lax.fori_loop(first, first + count, one, 0)

    part[...] = jnp.zeros_like(part)
    edges[0].wait_recv()
    edges[1].wait_recv()
    insert_edges(0)
    loads[2].wait()
    taps(2)
    to_peer(22, 10)

    for copy in halo[2:]:
        copy.wait_recv()
    edges[2].wait_recv()
    edges[3].wait_recv()
    for s in range(2, 4):
        zero_unless(row != 0, s, 0)
        zero_unless(row != 3, s, 17)

    @pl.when(tm == 3)
    def _():
        gx[1, pl.ds(2, 2)] = jnp.zeros((2, 18, 16, C), BF16)

    insert_edges(1)
    taps(1)
    taps(0)
    to_peer(0, 22)

    act_grad = part[1] + roll_w(part[2], True) + roll_w(part[0], False)
    feat = f_v[...].reshape(512, C).astype(F32)
    scale = lax.rsqrt(jnp.mean(feat * feat, axis=-1, keepdims=True) + EPS)
    unit = feat * scale
    normed = unit * gain
    sig = jax.nn.sigmoid(normed)
    normed_grad = act_grad * (sig * (1.0 + normed * (1.0 - sig)))
    gain_local = jnp.sum(normed_grad * unit, axis=0, keepdims=True)
    unit_grad = normed_grad * gain
    lean = jnp.mean(unit_grad * unit, axis=-1, keepdims=True)
    feat_grad = scale * (unit_grad - unit * lean)
    grad = gx[1, pl.ds(0, 2), pl.ds(1, 16)].reshape(512, C).astype(F32)
    ig[...] = (grad + feat_grad).astype(BF16).reshape(2, 16, 16, C)

    tokens = []
    for d in range(1, 16):
        there = lax.rem(col + d, 16)
        tokens.append(
            remote(
                ig.at[:, there],
                ig_out.at[:, 0, pl.ds(pl.multiple_of(16 * col, 16), 16)],
                a_ss.at[d - 1],
                a_rs.at[d - 1],
                moved(col=d),
            )
        )
    for copy in tokens:
        copy.start()
    ig_out[:, 0, pl.ds(pl.multiple_of(16 * col, 16), 16)] = ig[:, col]

    gs[0] = jnp.zeros((8, 128), F32)
    gs[0, pl.ds(0, 1), :] = gain_local[:, :128]
    gs[0, pl.ds(1, 1), pl.ds(0, 64)] = gain_local[:, 128:]
    gain_copies = []

    def gain_send(stage, slot, where):
        copy = remote(gs.at[stage], gr.at[slot], g_ss.at[slot], g_rs.at[slot], where)
        copy.start()
        gain_copies.append(copy)

    def gain_sum(stage, slots):
        total = gs[stage]
        for slot in slots:
            gain_copies[slot].wait_recv()
            total = total + gr[slot]
        return total

    gain_send(0, 0, peer)

    whole = pl.ds(0, 32 * 88)
    for i, (src, dst) in enumerate(((s_lo, r_lo), (s_hi, r_hi))):
        remote(src.at[whole], dst.at[whole], c_ss.at[i], c_rs.at[i], peer).wait()
    gs[1] = gain_sum(0, [0])
    for r in range(1, 4):
        gain_send(1, r, moved(row=r))

    lane = lax.broadcasted_iota(jnp.int32, (48, 128), 1)
    rows_copies = []
    for r in (2, 1, 3, 0):
        x = lax.rem(row + r, 4)

        def gather(z, carry, x=x):
            start = 81 * (16 * x + 2 * z + core)
            both = s_lo[pl.ds(start, 88), :] + r_lo[pl.ds(start, 88), :]
            ff[x, pl.ds(81 * z, 88), :] = both
            top = s_hi[pl.ds(start, 48), :] + r_hi[pl.ds(start, 48), :]
            low = s_hi[pl.ds(start + 41, 48), :] + r_hi[pl.ds(start + 41, 48), :]
            ff[x, pl.ds(656 + 41 * z, 48), :] = jnp.where(lane < 64, top, pltpu.roll(low, 64, 1))
            return carry

        lax.fori_loop(0, 8, gather, 0)
        if r:
            p1s[x] = ff[x].astype(BF16)
            copy = remote(p1s.at[x], p1r.at[r - 1], x_ss.at[r - 1], x_rs.at[r - 1], moved(row=r))
            copy.start()
            rows_copies.append(copy)
    for copy in rows_copies:
        copy.wait_recv()
    t_sum[...] = (
        ff[row] + p1r[0].astype(F32) + p1r[1].astype(F32) + p1r[2].astype(F32)
    )
    gs[2] = gain_sum(1, [1, 2, 3])
    for t in range(1, 4):
        gain_send(2, 3 + t, moved(tm=-t))

    def columns(z, carry):
        a = t_sum[pl.ds(81 * z, 48), :]
        b = t_sum[pl.ds(81 * z + 41, 48), :]
        h = t_sum[pl.ds(656 + 41 * z, 48), :]
        h32 = pltpu.roll(h, 32, 1)
        rows = pl.ds(41 * z, 48)
        vv[0, rows, :] = jnp.where(lane < 64, a, pltpu.roll(b, 64, 1))
        vv[1, rows, :] = jnp.where(lane < 64, pltpu.roll(a, 80, 1), pltpu.roll(b, 16, 1))
        left = jnp.where(lane < 32, pltpu.roll(a, 32, 1), h32)
        right = jnp.where(lane < 96, pltpu.roll(b, 96, 1), h32)
        vv[2, rows, :] = jnp.where(lane < 64, left, right)
        vv[3, rows, :] = pltpu.roll(h, 112, 1)
        return carry

    lax.fori_loop(0, 8, columns, 0)
    p2s[...] = vv[...].astype(BF16)
    column_copies = []
    for t in range(1, 4):
        y = lax.rem(tm + 4 - t, 4)
        copy = remote(p2s.at[y], p2r.at[t - 1], y_ss.at[t - 1], y_rs.at[t - 1], moved(tm=-t))
        copy.start()
        column_copies.append(copy)
    for copy in column_copies:
        copy.wait_recv()
    u_sum[...] = (
        vv[tm] + p2r[0].astype(F32) + p2r[1].astype(F32) + p2r[2].astype(F32)
    )
    gs[3] = gain_sum(2, [4, 5, 6])
    for d in range(1, 8):
        gain_send(3, 6 + d, moved(col=2 * d))
    for z in range(8):
        p3s[z] = u_sum[41 * z : 41 * z + 48]
    depth_copies = []
    for d in range(1, 8):
        z = lax.rem(zed + d, 8)
        copy = remote(p3s.at[z], p3r.at[d - 1], z_ss.at[d - 1], z_rs.at[d - 1], moved(col=2 * d))
        copy.start()
        depth_copies.append(copy)
    total = p3s[zed]
    for d in range(7):
        depth_copies[d].wait_recv()
        total = total + p3r[d]
    wg_out[pl.ds(0, 41), :] = total[:41, :48]
    wg_out[pl.ds(41, 40), :] = pltpu.roll(total, 64, 1)[:40, :48]
    gain_all = gain_sum(3, [7, 8, 9, 10, 11, 12, 13])
    gg_out[:, pl.ds(0, 128)] = gain_all[:1]
    gg_out[:, pl.ds(128, 64)] = gain_all[1:2, :64]

    for copy in tokens:
        copy.wait()
    for copy in halo + edges + rows_copies + column_copies + depth_copies + gain_copies:
        copy.wait_send()


def shards(features, norm_gain, conv_weight, out_grad):
    any_spec = pl.BlockSpec(memory_space=pl.ANY)
    vmem = pl.BlockSpec(memory_space=pltpu.VMEM)
    dma = pltpu.SemaphoreType.DMA
    scratch = [
        pltpu.VMEM((2, 16, 16, C), BF16),
        pltpu.VMEM((3, 4, 18, 16, C), BF16),
        pltpu.VMEM((27, C, C), BF16),
        pltpu.VMEM((2, 48, C), BF16),
        pltpu.VMEM((2, 2, 48, C), BF16),
        pltpu.VMEM((2, 48, C), F32),
        pltpu.VMEM((3, C, 512), BF16),
        pltpu.VMEM((3, 512, C), F32),
        pltpu.VMEM((5192, 128), F32),
        pltpu.VMEM((5192, 128), F32),
        pltpu.VMEM((5192, 128), F32),
        pltpu.VMEM((5192, 128), F32),
        pltpu.VMEM((4, 992, 128), F32),
        pltpu.VMEM((4, 992, 128), BF16),
        pltpu.VMEM((3, 992, 128), BF16),
        pltpu.VMEM((992, 128), F32),
        pltpu.VMEM((4, 336, 128), F32),
        pltpu.VMEM((4, 336, 128), BF16),
        pltpu.VMEM((3, 336, 128), BF16),
        pltpu.VMEM((336, 128), F32),
        pltpu.VMEM((8, 48, 128), F32),
        pltpu.VMEM((7, 48, 128), F32),
        pltpu.VMEM((4, 8, 128), F32),
        pltpu.VMEM((14, 8, 128), F32),
        pltpu.VMEM((2, 16, 16, C), BF16),
        dma((3,)),
        dma((5,)), dma((5,)),
        dma((4,)), dma((4,)),
        dma((2,)), dma((2,)),
        dma((3,)), dma((3,)),
        dma((3,)), dma((3,)),
        dma((7,)), dma((7,)),
        dma((15,)), dma((15,)),
        dma((14,)), dma((14,)),
    ]
    ig, wg, gg = pl.pallas_call(
        kernel,
        out_shape=(
            jax.ShapeDtypeStruct((2, 1, 256, C), BF16),
            jax.ShapeDtypeStruct((81, 48), F32),
            jax.ShapeDtypeStruct((1, C), F32),
        ),
        in_specs=[any_spec, vmem, any_spec, any_spec],
        out_specs=(vmem, vmem, vmem),
        scratch_shapes=scratch,
        compiler_params=pltpu.CompilerParams(
            collective_id=0, has_side_effects=True, vmem_limit_bytes=56 * 2**20
        ),
        name="unit_backward",
    )(features, norm_gain.reshape(1, C), conv_weight.reshape(27, C, C), out_grad)
    return ig, wg, gg.reshape(C)


def solution(mesh):
    in_specs = (P("tm", "row", "col", None), P(), P(), P("tm", "row", "col", None))
    out_specs = (P("tm", ("row", "col"), None, None), P(("row", "col"), "tm"), P())
    return jax.shard_map(shards, mesh=mesh, in_specs=in_specs, out_specs=out_specs, check_vma=False)
```

```python
import jax
import jax.numpy as jnp
from jax import lax
from jax.experimental import pallas as pl
from jax.experimental.pallas import tpu as pltpu
from jax.sharding import PartitionSpec as P

MESH = pl.DeviceIdType.MESH
AXES = ("tm", "row", "col")
SIZES = (4, 4, 16)
F32 = jnp.float32
BF16 = jnp.bfloat16
C = 192
EPS = 1e-06


def moved(tm=0, row=0, col=0):
    out = []
    for name, size, off in zip(AXES, SIZES, (tm, row, col)):
        out.append(lax.rem(lax.axis_index(name) + (off % size), size))
    return tuple(out)


REACHED = (
    [(-1, 0, 0), (-2, 0, 0), (-3, 0, 0)]
    + [(0, r, 0) for r in (1, 2, 3)]
    + [(-1, 1, 0), (-1, -1, 0), (-1, 0, 1), (-1, 0, -1)]
    + [(0, 0, d) for d in range(1, 16)]
)


def roll_w(x, forward):
    rows = x.shape[0]
    place = lax.rem(lax.broadcasted_iota(jnp.int32, x.shape, 0), 16)
    if forward:
        return jnp.where(place == 0, pltpu.roll(x, rows - 15, 0), pltpu.roll(x, 1, 0))
    return jnp.where(place == 15, pltpu.roll(x, 15, 0), pltpu.roll(x, rows - 1, 0))


def kernel(
    feat_hbm, gain_ref, w_hbm, grad_hbm,
    ig_out, wg_out, gg_out,
    f_v, gx, wt_v, w_v, e_s, e_r, e32, act_t, part, s_lo, s_hi, r_lo, r_hi,
    ff, p1s, p1r, t_sum, vv, p2s, p2r, u_sum, p3s, p3r, gs, gr, ig,
    loc_sem, h_ss, h_rs, e_ss, e_rs, c_ss, c_rs, x_ss, x_rs, y_ss, y_rs, z_ss, z_rs,
    a_ss, a_rs, g_ss, g_rs,
):
    tm, row, col = (lax.axis_index(a) for a in AXES)
    core = lax.rem(col, 2)
    zed = col // 2
    peer = (tm, row, col + 1 - 2 * core)

    loads = [
        pltpu.make_async_copy(feat_hbm, f_v, loc_sem.at[0]),
        pltpu.make_async_copy(grad_hbm, gx.at[1, pl.ds(0, 2), pl.ds(1, 16)], loc_sem.at[1]),
        pltpu.make_async_copy(w_hbm, wt_v, loc_sem.at[2]),
    ]
    for load in loads:
        load.start()

    barrier = pltpu.get_barrier_semaphore()
    for off in REACHED:
        pl.semaphore_signal(
            barrier, inc=1, device_id=moved(*[-o for o in off]), device_id_type=MESH
        )
    pl.semaphore_wait(barrier, len(REACHED))

    def remote(src, dst, ss, rs, where):
        return pltpu.make_async_remote_copy(
            src_ref=src, dst_ref=dst, send_sem=ss, recv_sem=rs, device_id=where, device_id_type=MESH
        )

    halo = [
        remote(grad_hbm.at[:, 15], gx.at[1, pl.ds(0, 2), 0], h_ss.at[0], h_rs.at[0], moved(row=1)),
        remote(grad_hbm.at[:, 0], gx.at[1, pl.ds(0, 2), 17], h_ss.at[1], h_rs.at[1], moved(row=-1)),
        remote(grad_hbm.at[:, 15], gx.at[1, pl.ds(2, 2), 0], h_ss.at[2], h_rs.at[2], moved(tm=-1, row=1)),
        remote(grad_hbm.at[:, 0], gx.at[1, pl.ds(2, 2), 17], h_ss.at[3], h_rs.at[3], moved(tm=-1, row=-1)),
        remote(grad_hbm.at[0], gx.at[1, 2, pl.ds(1, 16)], h_ss.at[4], h_rs.at[4], moved(tm=-1)),
        remote(grad_hbm.at[1], gx.at[1, 3, pl.ds(1, 16)], h_ss.at[5], h_rs.at[5], moved(tm=-1)),
    ]
    for copy in halo:
        copy.start()

    gain = gain_ref[...]
    loads[0].wait()
    feat = f_v[...].reshape(512, C).astype(F32)
    scale = lax.rsqrt(jnp.mean(feat * feat, axis=-1, keepdims=True) + EPS)
    normed = feat * scale * gain
    act = normed * jax.nn.sigmoid(normed)
    act = act.astype(BF16).astype(F32)
    wide = jnp.concatenate([act, jnp.zeros((512, 64), F32)], axis=1)
    for kw in range(3):
        turned = wide if kw == 1 else roll_w(wide, kw == 0)
        act_t[kw] = jnp.transpose(turned)[:C].astype(BF16)

    def take_edges(dt):
        for side, edge in ((0, 0), (1, 15)):
            keep = col != edge
            if dt == 1:
                keep = jnp.logical_and(keep, tm != 3)
            e32[side] = jnp.where(keep, e_r[side, dt].astype(F32), 0.0)

    def insert_edges(s):
        place = lax.broadcasted_iota(jnp.int32, (16, C), 0)
        for h in range(18):
            n = 18 * (s % 2) + h
            mid = gx[1, s, h].astype(F32)
            left = jnp.broadcast_to(e32[0, n : n + 1, :], (16, C))
            right = jnp.broadcast_to(e32[1, n : n + 1, :], (16, C))
            gx[2, s, h] = jnp.where(place == 15, left, mid).astype(BF16)
            gx[0, s, h] = jnp.where(place == 0, right, mid).astype(BF16)

    def zero_unless(keep, s, h):
        gx[1, s, h] = jnp.where(keep, gx[1, s, h].astype(F32), 0.0).astype(BF16)

    loads[1].wait()
    halo[0].wait_recv()
    halo[1].wait_recv()
    for s in range(2):
        zero_unless(row != 0, s, 0)
        zero_unless(row != 3, s, 17)
    own = gx[1, pl.ds(0, 2)].reshape(576, C)
    for side, place in ((0, 15), (1, 0)):
        r = lax.broadcasted_iota(jnp.int32, (48, 576), 0)
        q = lax.broadcasted_iota(jnp.int32, (48, 576), 1)
        pick = jnp.where(jnp.logical_and(q == 16 * r + place, r < 36), 1.0, 0.0).astype(BF16)
        e_s[side] = jnp.dot(pick, own, preferred_element_type=F32).astype(BF16)
    edges = []
    for dt in range(2):
        for side, step in ((0, 1), (1, -1)):
            i = 2 * dt + side
            edges.append(
                remote(e_s.at[side], e_r.at[side, dt], e_ss.at[i], e_rs.at[i], moved(tm=-dt, col=step))
            )
    for copy in edges:
        copy.start()

    def taps(kt):
        for kw in range(3):
            total = None if kt == 2 else part[kw]
            for kh in range(3):
                k = 9 * kt + 3 * kh + kw
                cells = gx[kw, 2 - kt : 4 - kt, 2 - kh : 18 - kh].reshape(512, C)
                more = jnp.dot(cells, w_v[k], preferred_element_type=F32)
                total = more if total is None else total + more
                wg = jnp.dot(act_t[kw], cells, preferred_element_type=F32)
                s_lo[192 * k : 192 * k + 192, :] = wg[:, :128]
                s_hi[192 * k : 192 * k + 192, 0:64] = wg[:, 128:]
            part[kw] = total

    def to_peer(first, count, chunk):
        def one(m, carry):
            start = pl.multiple_of((81 * (2 * m + 1 - core)) // 8 * 8, 8)
            rows = pl.ds(start, 88)
            remote(s_lo.at[rows], r_lo.at[rows], c_ss.at[2 * chunk], c_rs.at[2 * chunk], peer).start()
            remote(s_hi.at[rows], r_hi.at[rows], c_ss.at[2 * chunk + 1], c_rs.at[2 * chunk + 1], peer).start()
            return carry

        lax.fori_loop(first, first + count, one, 0)

    loads[2].wait()
    for k in range(27):
        w_v[k] = wt_v[:, 192 * k : 192 * k + 192]
    edges[0].wait_recv()
    edges[1].wait_recv()
    take_edges(0)
    insert_edges(0)
    insert_edges(1)
    taps(2)
    to_peer(22, 10, 0)

    edges[2].wait_recv()
    edges[3].wait_recv()
    take_edges(1)
    halo[2].wait_recv()
    halo[3].wait_recv()
    for s in (2, 3):
        halo[s + 2].wait_recv()
        zero_unless(row != 0, s, 0)
        zero_unless(row != 3, s, 17)

        @pl.when(tm == 3)
        def _(s=s):
            gx[1, s] = jnp.zeros((18, 16, C), BF16)

        insert_edges(s)
        taps(3 - s)
        if s == 2:
            to_peer(11, 11, 1)
        else:
            to_peer(0, 11, 2)

    act_grad = part[1] + roll_w(part[2], True) + roll_w(part[0], False)
    feat = f_v[...].reshape(512, C).astype(F32)
    scale = lax.rsqrt(jnp.mean(feat * feat, axis=-1, keepdims=True) + EPS)
    unit = feat * scale
    normed = unit * gain
    sig = jax.nn.sigmoid(normed)
    normed_grad = act_grad * (sig * (1.0 + normed * (1.0 - sig)))
    gain_local = jnp.sum(normed_grad * unit, axis=0, keepdims=True)
    unit_grad = normed_grad * gain
    lean = jnp.mean(unit_grad * unit, axis=-1, keepdims=True)
    feat_grad = scale * (unit_grad - unit * lean)
    grad = gx[1, pl.ds(0, 2), pl.ds(1, 16)].reshape(512, C).astype(F32)
    ig[...] = (grad + feat_grad).astype(BF16).reshape(2, 16, 16, C)

    tokens = []
    for d in range(1, 16):
        there = lax.rem(col + d, 16)
        tokens.append(
            remote(
                ig.at[:, there],
                ig_out.at[:, pl.ds(pl.multiple_of(16 * col, 16), 16)],
                a_ss.at[d - 1],
                a_rs.at[d - 1],
                moved(col=d),
            )
        )
    for copy in tokens:
        copy.start()
    ig_out[:, pl.ds(pl.multiple_of(16 * col, 16), 16)] = ig[:, col]

    gs[0] = jnp.zeros((8, 128), F32)
    gs[0, pl.ds(0, 1), :] = gain_local[:, :128]
    gs[0, pl.ds(1, 1), pl.ds(0, 64)] = gain_local[:, 128:]
    gain_copies = []

    def gain_send(stage, slot, where):
        copy = remote(gs.at[stage], gr.at[slot], g_ss.at[slot], g_rs.at[slot], where)
        copy.start()
        gain_copies.append(copy)

    def gain_sum(stage, slots):
        total = gs[stage]
        for slot in slots:
            gain_copies[slot].wait_recv()
            total = total + gr[slot]
        return total

    gain_send(0, 0, peer)

    for chunk, count in enumerate((10, 11, 11)):
        whole = pl.ds(0, count * 88)
        for i, (src, dst) in enumerate(((s_lo, r_lo), (s_hi, r_hi))):
            sem = 2 * chunk + i
            remote(src.at[whole], dst.at[whole], c_ss.at[sem], c_rs.at[sem], peer).wait()
    gs[1] = gain_sum(0, [0])
    for r in range(1, 4):
        gain_send(1, r, moved(row=r))

    lane = lax.broadcasted_iota(jnp.int32, (48, 128), 1)
    rows_copies = []
    for r in (2, 1, 3, 0):
        x = lax.rem(row + r, 4)

        def gather(z, carry, x=x):
            start = 81 * (16 * x + 2 * z + core)
            both = s_lo[pl.ds(start, 88), :] + r_lo[pl.ds(start, 88), :]
            ff[x, pl.ds(81 * z, 88), :] = both
            top = s_hi[pl.ds(start, 48), :] + r_hi[pl.ds(start, 48), :]
            low = s_hi[pl.ds(start + 41, 48), :] + r_hi[pl.ds(start + 41, 48), :]
            ff[x, pl.ds(656 + 41 * z, 48), :] = jnp.where(lane < 64, top, pltpu.roll(low, 64, 1))
            return carry

        lax.fori_loop(0, 8, gather, 0)
        if r:
            p1s[x] = ff[x].astype(BF16)
            copy = remote(p1s.at[x], p1r.at[r - 1], x_ss.at[r - 1], x_rs.at[r - 1], moved(row=r))
            copy.start()
            rows_copies.append(copy)
    for copy in rows_copies:
        copy.wait_recv()
    t_sum[...] = (
        ff[row] + p1r[0].astype(F32) + p1r[1].astype(F32) + p1r[2].astype(F32)
    )
    gs[2] = gain_sum(1, [1, 2, 3])
    for t in range(1, 4):
        gain_send(2, 3 + t, moved(tm=-t))

    def columns(z, carry):
        a = t_sum[pl.ds(81 * z, 48), :]
        b = t_sum[pl.ds(81 * z + 41, 48), :]
        h = t_sum[pl.ds(656 + 41 * z, 48), :]
        h32 = pltpu.roll(h, 32, 1)
        rows = pl.ds(41 * z, 48)
        vv[0, rows, :] = jnp.where(lane < 64, a, pltpu.roll(b, 64, 1))
        vv[1, rows, :] = jnp.where(lane < 64, pltpu.roll(a, 80, 1), pltpu.roll(b, 16, 1))
        left = jnp.where(lane < 32, pltpu.roll(a, 32, 1), h32)
        right = jnp.where(lane < 96, pltpu.roll(b, 96, 1), h32)
        vv[2, rows, :] = jnp.where(lane < 64, left, right)
        vv[3, rows, :] = pltpu.roll(h, 112, 1)
        return carry

    lax.fori_loop(0, 8, columns, 0)
    p2s[...] = vv[...].astype(BF16)
    column_copies = []
    for t in range(1, 4):
        y = lax.rem(tm + 4 - t, 4)
        copy = remote(p2s.at[y], p2r.at[t - 1], y_ss.at[t - 1], y_rs.at[t - 1], moved(tm=-t))
        copy.start()
        column_copies.append(copy)
    for copy in column_copies:
        copy.wait_recv()
    u_sum[...] = (
        vv[tm] + p2r[0].astype(F32) + p2r[1].astype(F32) + p2r[2].astype(F32)
    )
    gs[3] = gain_sum(2, [4, 5, 6])
    for d in range(1, 8):
        gain_send(3, 6 + d, moved(col=2 * d))
    for z in range(8):
        p3s[z] = u_sum[41 * z : 41 * z + 48]
    depth_copies = []
    for d in range(1, 8):
        z = lax.rem(zed + d, 8)
        copy = remote(p3s.at[z], p3r.at[d - 1], z_ss.at[d - 1], z_rs.at[d - 1], moved(col=2 * d))
        copy.start()
        depth_copies.append(copy)
    total = p3s[zed]
    for d in range(7):
        depth_copies[d].wait_recv()
        total = total + p3r[d]
    wg_out[...] = total
    gg_out[...] = gain_sum(3, [7, 8, 9, 10, 11, 12, 13])

    for copy in tokens:
        copy.wait()
    for copy in halo + edges + rows_copies + column_copies + depth_copies + gain_copies:
        copy.wait_send()


def finish(ig_ref, wg_ref, gg_ref, ig_out, wg_out, gg_out):
    for f in range(2):
        wide = jnp.concatenate([ig_ref[f].astype(F32), jnp.zeros((256, 64), F32)], axis=1)
        ig_out[f] = jnp.transpose(wide)[:C].astype(BF16)
    square = jnp.concatenate([wg_ref[...], jnp.zeros((80, 128), F32)], axis=0)
    turned = jnp.transpose(square)
    wg_out[:, 0:41] = turned[0:48, 0:41]
    wg_out[:, 41:81] = turned[64:112, 0:40]
    gg_out[:, 0:128] = gg_ref[0:1]
    gg_out[:, 128:192] = gg_ref[1:2, 0:64]


def shards(features, norm_gain, conv_weight, out_grad):
    any_spec = pl.BlockSpec(memory_space=pl.ANY)
    vmem = pl.BlockSpec(memory_space=pltpu.VMEM)
    dma = pltpu.SemaphoreType.DMA
    scratch = [
        pltpu.VMEM((2, 16, 16, C), BF16),
        pltpu.VMEM((3, 4, 18, 16, C), BF16),
        pltpu.VMEM((C, 27 * C), BF16),
        pltpu.VMEM((27, C, C), BF16),
        pltpu.VMEM((2, 48, C), BF16),
        pltpu.VMEM((2, 2, 48, C), BF16),
        pltpu.VMEM((2, 48, C), F32),
        pltpu.VMEM((3, C, 512), BF16),
        pltpu.VMEM((3, 512, C), F32),
        pltpu.VMEM((5192, 128), F32),
        pltpu.VMEM((5192, 128), F32),
        pltpu.VMEM((5192, 128), F32),
        pltpu.VMEM((5192, 128), F32),
        pltpu.VMEM((4, 992, 128), F32),
        pltpu.VMEM((4, 992, 128), BF16),
        pltpu.VMEM((3, 992, 128), BF16),
        pltpu.VMEM((992, 128), F32),
        pltpu.VMEM((4, 336, 128), F32),
        pltpu.VMEM((4, 336, 128), BF16),
        pltpu.VMEM((3, 336, 128), BF16),
        pltpu.VMEM((336, 128), F32),
        pltpu.VMEM((8, 48, 128), F32),
        pltpu.VMEM((7, 48, 128), F32),
        pltpu.VMEM((4, 8, 128), F32),
        pltpu.VMEM((14, 8, 128), F32),
        pltpu.VMEM((2, 16, 16, C), BF16),
        dma((3,)),
        dma((6,)), dma((6,)),
        dma((4,)), dma((4,)),
        dma((6,)), dma((6,)),
        dma((3,)), dma((3,)),
        dma((3,)), dma((3,)),
        dma((7,)), dma((7,)),
        dma((15,)), dma((15,)),
        dma((14,)), dma((14,)),
    ]
    ig, wg, gg = pl.pallas_call(
        kernel,
        out_shape=(
            jax.ShapeDtypeStruct((2, 256, C), BF16),
            jax.ShapeDtypeStruct((48, 128), F32),
            jax.ShapeDtypeStruct((8, 128), F32),
        ),
        in_specs=[any_spec, vmem, any_spec, any_spec],
        out_specs=(vmem, vmem, vmem),
        scratch_shapes=scratch,
        compiler_params=pltpu.CompilerParams(
            collective_id=0, has_side_effects=True, vmem_limit_bytes=56 * 2**20
        ),
        name="unit_backward",
    )(features, norm_gain.reshape(1, C), conv_weight.T, out_grad)
    ig, wg, gg = pl.pallas_call(
        finish,
        out_shape=(
            jax.ShapeDtypeStruct((2, C, 256), BF16),
            jax.ShapeDtypeStruct((48, 81), F32),
            jax.ShapeDtypeStruct((1, C), F32),
        ),
        in_specs=[vmem, vmem, vmem],
        out_specs=(vmem, vmem, vmem),
        name="finish",
    )(ig, wg, gg)
    return ig.transpose(0, 2, 1)[:, None], wg.T, gg.reshape(C)


def solution(mesh):
    in_specs = (P("tm", "row", "col", None), P(), P(), P("tm", "row", "col", None))
    out_specs = (P("tm", ("row", "col"), None, None), P(("row", "col"), "tm"), P())
    return jax.shard_map(shards, mesh=mesh, in_specs=in_specs, out_specs=out_specs, check_vma=False)
```

```python
import jax
import jax.numpy as jnp
from jax import lax
from jax.experimental import pallas as pl
from jax.experimental.pallas import tpu as pltpu
from jax.sharding import PartitionSpec as P

MESH = pl.DeviceIdType.MESH
AXES = ("tm", "row", "col")
SIZES = (4, 4, 16)
F32 = jnp.float32
BF16 = jnp.bfloat16
C = 192
EPS = 1e-06
NA = 5
NB = 8 - NA
HALF = 41


def tiles(rows, unit=16):
    return -(-rows // unit) * unit


LO = tiles(81 * (NA - 1) + 88)
HI = tiles(HALF * (NA - 1) + 48)
A1 = LO + HI
B1 = tiles(4 * NB * HALF)
B1_SCRATCH = tiles(HALF * (4 * NB - 1) + 48, 8)
A2 = tiles(NA * HALF)
A2_SCRATCH = tiles(HALF * (NA - 1) + 48, 8)
B2 = tiles(NB * HALF)
B2_SCRATCH = tiles(HALF * (NB - 1) + 48, 8)
PEER_CHUNKS = ((22, 10), (11, 11), (8, 3), (4, 4), (0, 4))


def moved(tm=0, row=0, col=0):
    out = []
    for name, size, off in zip(AXES, SIZES, (tm, row, col)):
        out.append(lax.rem(lax.axis_index(name) + (off % size), size))
    return tuple(out)


REACHED = (
    [(-1, 0, 0), (-2, 0, 0), (-3, 0, 0)]
    + [(0, r, 0) for r in (1, 2, 3)]
    + [(-1, 1, 0), (-1, -1, 0), (-1, 0, 1), (-1, 0, -1)]
    + [(0, 0, d) for d in range(1, 16)]
)


def roll_w(x, forward):
    rows = x.shape[0]
    place = lax.rem(lax.broadcasted_iota(jnp.int32, x.shape, 0), 16)
    if forward:
        return jnp.where(place == 0, pltpu.roll(x, rows - 15, 0), pltpu.roll(x, 1, 0))
    return jnp.where(place == 15, pltpu.roll(x, 15, 0), pltpu.roll(x, rows - 1, 0))


def kernel(
    feat_hbm, gain_ref, w_hbm, grad_hbm,
    ig_out, wg_out, gg_out,
    f_v, gx, wt_v, w_v, e_s, e_r, e32, act_t, part, s_lo, s_hi, r_lo, r_hi,
    ffa, p1a_s, p1a_r, t_a, vb, p1b_s, p1b_r, t_b, va, p2a_s, p2a_r, u_a, p2b_s, p2b_r, u_b,
    p3s, p3r, gs, gr, ig,
    loc_sem, h_ss, h_rs, e_ss, e_rs, c_ss, c_rs, x_ss, x_rs, y_ss, y_rs, x2_ss, x2_rs, y2_ss, y2_rs, z_ss, z_rs,
    a_ss, a_rs, g_ss, g_rs,
):
    tm, row, col = (lax.axis_index(a) for a in AXES)
    core = lax.rem(col, 2)
    zed = col // 2
    peer = (tm, row, col + 1 - 2 * core)

    loads = [
        pltpu.make_async_copy(feat_hbm, f_v, loc_sem.at[0]),
        pltpu.make_async_copy(grad_hbm, gx.at[1, pl.ds(0, 2), pl.ds(1, 16)], loc_sem.at[1]),
        pltpu.make_async_copy(w_hbm, wt_v, loc_sem.at[2]),
    ]
    for load in loads:
        load.start()

    barrier = pltpu.get_barrier_semaphore()
    for off in REACHED:
        pl.semaphore_signal(
            barrier, inc=1, device_id=moved(*[-o for o in off]), device_id_type=MESH
        )
    pl.semaphore_wait(barrier, len(REACHED))

    def remote(src, dst, ss, rs, where):
        return pltpu.make_async_remote_copy(
            src_ref=src, dst_ref=dst, send_sem=ss, recv_sem=rs, device_id=where, device_id_type=MESH
        )

    halo = [
        remote(grad_hbm.at[:, 15], gx.at[1, pl.ds(0, 2), 0], h_ss.at[0], h_rs.at[0], moved(row=1)),
        remote(grad_hbm.at[:, 0], gx.at[1, pl.ds(0, 2), 17], h_ss.at[1], h_rs.at[1], moved(row=-1)),
        remote(grad_hbm.at[:, 15], gx.at[1, pl.ds(2, 2), 0], h_ss.at[2], h_rs.at[2], moved(tm=-1, row=1)),
        remote(grad_hbm.at[:, 0], gx.at[1, pl.ds(2, 2), 17], h_ss.at[3], h_rs.at[3], moved(tm=-1, row=-1)),
        remote(grad_hbm.at[0], gx.at[1, 2, pl.ds(1, 16)], h_ss.at[4], h_rs.at[4], moved(tm=-1)),
        remote(grad_hbm.at[1], gx.at[1, 3, pl.ds(1, 16)], h_ss.at[5], h_rs.at[5], moved(tm=-1)),
    ]
    for copy in halo:
        copy.start()

    gain = gain_ref[...]
    loads[0].wait()
    feat = f_v[...].reshape(512, C).astype(F32)
    scale = lax.rsqrt(jnp.mean(feat * feat, axis=-1, keepdims=True) + EPS)
    normed = feat * scale * gain
    act = normed * jax.nn.sigmoid(normed)
    act = act.astype(BF16).astype(F32)
    wide = jnp.concatenate([act, jnp.zeros((512, 64), F32)], axis=1)
    for kw in range(3):
        turned = wide if kw == 1 else roll_w(wide, kw == 0)
        act_t[kw] = jnp.transpose(turned)[:C].astype(BF16)

    def take_edges(dt):
        for side, edge in ((0, 0), (1, 15)):
            keep = col != edge
            if dt == 1:
                keep = jnp.logical_and(keep, tm != 3)
            e32[side] = jnp.where(keep, e_r[side, dt].astype(F32), 0.0)

    def insert_edges(s):
        place = lax.broadcasted_iota(jnp.int32, (16, C), 0)
        for h in range(18):
            n = 18 * (s % 2) + h
            mid = gx[1, s, h].astype(F32)
            left = jnp.broadcast_to(e32[0, n : n + 1, :], (16, C))
            right = jnp.broadcast_to(e32[1, n : n + 1, :], (16, C))
            gx[2, s, h] = jnp.where(place == 15, left, mid).astype(BF16)
            gx[0, s, h] = jnp.where(place == 0, right, mid).astype(BF16)

    def zero_unless(keep, s, h):
        gx[1, s, h] = jnp.where(keep, gx[1, s, h].astype(F32), 0.0).astype(BF16)

    loads[1].wait()
    halo[0].wait_recv()
    halo[1].wait_recv()
    for s in range(2):
        zero_unless(row != 0, s, 0)
        zero_unless(row != 3, s, 17)
    own = gx[1, pl.ds(0, 2)].reshape(576, C)
    for side, place in ((0, 15), (1, 0)):
        r = lax.broadcasted_iota(jnp.int32, (48, 576), 0)
        q = lax.broadcasted_iota(jnp.int32, (48, 576), 1)
        pick = jnp.where(jnp.logical_and(q == 16 * r + place, r < 36), 1.0, 0.0).astype(BF16)
        e_s[side] = jnp.dot(pick, own, preferred_element_type=F32).astype(BF16)
    edges = []
    for dt in range(2):
        for side, step in ((0, 1), (1, -1)):
            i = 2 * dt + side
            edges.append(
                remote(e_s.at[side], e_r.at[side, dt], e_ss.at[i], e_rs.at[i], moved(tm=-dt, col=step))
            )
    for copy in edges:
        copy.start()

    def cells_of(kt, kh, kw):
        return gx[kw, 2 - kt : 4 - kt, 2 - kh : 18 - kh].reshape(512, C)

    def weight_taps(kt, kh):
        for kw in range(3):
            k = 9 * kt + 3 * kh + kw
            wg = jnp.dot(act_t[kw], cells_of(kt, kh, kw), preferred_element_type=F32)
            s_lo[192 * k : 192 * k + 192, :] = wg[:, :128]
            s_hi[192 * k : 192 * k + 192, 0:64] = wg[:, 128:]

    def to_peer(chunk):
        def one(m, carry):
            start = pl.multiple_of((81 * (2 * m + 1 - core)) // 8 * 8, 8)
            rows = pl.ds(start, 88)
            for i, (src, dst) in enumerate(((s_lo, r_lo), (s_hi, r_hi))):
                sem = 2 * chunk + i
                remote(src.at[rows], dst.at[rows], c_ss.at[sem], c_rs.at[sem], peer).start()
            return carry

        first, count = PEER_CHUNKS[chunk]
        lax.fori_loop(first, first + count, one, 0)

    def peer_chunk(chunk):
        whole = pl.ds(0, PEER_CHUNKS[chunk][1] * 88)
        return [
            remote(src.at[whole], dst.at[whole], c_ss.at[2 * chunk + i], c_rs.at[2 * chunk + i], peer)
            for i, (src, dst) in enumerate(((s_lo, r_lo), (s_hi, r_hi)))
        ]

    lane = lax.broadcasted_iota(jnp.int32, (48, 128), 1)

    def slices(a, b, top, low):
        left = jnp.where(lane < 32, pltpu.roll(a, 32, 1), pltpu.roll(top, 32, 1))
        right = jnp.where(lane < 96, pltpu.roll(b, 96, 1), pltpu.roll(low, 96, 1))
        return (
            jnp.where(lane < 64, a, pltpu.roll(b, 64, 1)),
            jnp.where(lane < 64, pltpu.roll(a, 80, 1), pltpu.roll(b, 16, 1)),
            jnp.where(lane < 64, left, right),
            jnp.where(lane < 64, pltpu.roll(top, 112, 1), pltpu.roll(low, 48, 1)),
        )

    def gather(x):
        def both(own, other, start, rows):
            return own[pl.ds(start, rows), :] + other[pl.ds(start, rows), :]

        for z in range(8):
            start = 81 * (16 * x + 2 * z) + 81 * core
            top = both(s_hi, r_hi, start, 48)
            low = both(s_hi, r_hi, start + HALF, 48)
            if z < NA:
                ffa[x, 81 * z : 81 * z + 88, :] = both(s_lo, r_lo, start, 88)
                folded = jnp.where(lane < 64, top, pltpu.roll(low, 64, 1))
                ffa[x, LO + HALF * z : LO + HALF * z + 48, :] = folded
            else:
                a = both(s_lo, r_lo, start, 48)
                b = both(s_lo, r_lo, start + HALF, 48)
                at = HALF * (NB * x + z - NA)
                kept = 48 if z < 7 else HALF
                for y, piece in enumerate(slices(a, b, top, low)):
                    vb[y, at : at + kept, :] = piece[:kept]
        p1a_s[x] = ffa[x].astype(BF16)
        r = lax.rem(x + 4 - row, 4)

        @pl.when(r != 0)
        def _():
            remote(
                p1a_s.at[x], p1a_r.at[r - 1], x_ss.at[r - 1], x_rs.at[r - 1], (tm, x, col)
            ).start()

    loads[2].wait()
    for k in range(27):
        w_v[k] = wt_v[:, 192 * k : 192 * k + 192]
    edges[0].wait_recv()
    edges[1].wait_recv()
    take_edges(0)
    insert_edges(0)
    insert_edges(1)
    for kh in range(3):
        weight_taps(2, kh)
    to_peer(0)

    edges[2].wait_recv()
    edges[3].wait_recv()
    take_edges(1)
    halo[2].wait_recv()
    halo[3].wait_recv()
    for s in (2, 3):
        halo[s + 2].wait_recv()
        zero_unless(row != 0, s, 0)
        zero_unless(row != 3, s, 17)

        @pl.when(tm == 3)
        def _(s=s):
            gx[1, s] = jnp.zeros((18, 16, C), BF16)

        insert_edges(s)
        if s == 2:
            for kh in range(3):
                weight_taps(1, kh)
            to_peer(1)
            for copy in peer_chunk(0):
                copy.wait_recv()
            gather(3)
        else:
            weight_taps(0, 2)
            to_peer(2)
            weight_taps(0, 1)
            to_peer(3)
            weight_taps(0, 0)
            to_peer(4)

    for copy in peer_chunk(1):
        copy.wait_recv()
    gather(2)
    for copy in peer_chunk(2):
        copy.wait_recv()
    gather(1)
    for chunk in (3, 4):
        for copy in peer_chunk(chunk):
            copy.wait_recv()
    gather(0)
    column_copies = []
    for t in (2, 1, 3):
        y = lax.rem(tm + t, 4)
        p1b_s[y] = vb[y, 0:B1].astype(BF16)
        copy = remote(
            p1b_s.at[y], p1b_r.at[t - 1], y_ss.at[t - 1], y_rs.at[t - 1], moved(tm=t)
        )
        copy.start()
        column_copies.append(copy)

    for kw in range(3):
        total = None
        for kt in range(3):
            for kh in range(3):
                more = jnp.dot(
                    cells_of(kt, kh, kw), w_v[9 * kt + 3 * kh + kw], preferred_element_type=F32
                )
                total = more if total is None else total + more
        part[kw] = total

    act_grad = part[1] + roll_w(part[2], True) + roll_w(part[0], False)
    feat = f_v[...].reshape(512, C).astype(F32)
    scale = lax.rsqrt(jnp.mean(feat * feat, axis=-1, keepdims=True) + EPS)
    unit = feat * scale
    normed = unit * gain
    sig = jax.nn.sigmoid(normed)
    normed_grad = act_grad * (sig * (1.0 + normed * (1.0 - sig)))
    gain_local = jnp.sum(normed_grad * unit, axis=0, keepdims=True)
    unit_grad = normed_grad * gain
    lean = jnp.mean(unit_grad * unit, axis=-1, keepdims=True)
    feat_grad = scale * (unit_grad - unit * lean)
    grad = gx[1, pl.ds(0, 2), pl.ds(1, 16)].reshape(512, C).astype(F32)
    ig[...] = (grad + feat_grad).astype(BF16).reshape(2, 16, 16, C)

    tokens = []
    for d in range(1, 16):
        there = lax.rem(col + d, 16)
        tokens.append(
            remote(
                ig.at[:, there],
                ig_out.at[:, pl.ds(pl.multiple_of(16 * col, 16), 16)],
                a_ss.at[d - 1],
                a_rs.at[d - 1],
                moved(col=d),
            )
        )
    for copy in tokens:
        copy.start()
    ig_out[:, pl.ds(pl.multiple_of(16 * col, 16), 16)] = ig[:, col]

    gs[0] = jnp.zeros((8, 128), F32)
    gs[0, pl.ds(0, 1), :] = gain_local[:, :128]
    gs[0, pl.ds(1, 1), pl.ds(0, 64)] = gain_local[:, 128:]
    gain_copies = []

    def gain_send(stage, slot, where):
        copy = remote(gs.at[stage], gr.at[slot], g_ss.at[slot], g_rs.at[slot], where)
        copy.start()
        gain_copies.append(copy)

    def gain_sum(stage, slots):
        total = gs[stage]
        for slot in slots:
            gain_copies[slot].wait_recv()
            total = total + gr[slot]
        return total

    gain_send(0, 0, peer)

    gs[1] = gain_sum(0, [0])
    for r in range(1, 4):
        gain_send(1, r, moved(row=r))

    first_rows = [
        remote(p1a_s.at[r], p1a_r.at[r - 1], x_ss.at[r - 1], x_rs.at[r - 1], moved(row=r))
        for r in (1, 2, 3)
    ]
    for copy in first_rows:
        copy.wait_recv()
    t_a[...] = ffa[row] + p1a_r[0].astype(F32) + p1a_r[1].astype(F32) + p1a_r[2].astype(F32)
    for z in range(NA):
        a = t_a[81 * z : 81 * z + 48, :]
        b = t_a[81 * z + HALF : 81 * z + HALF + 48, :]
        top = t_a[LO + HALF * z : LO + HALF * z + 48, :]
        for y, piece in enumerate(slices(a, b, top, pltpu.roll(top, 64, 1))):
            va[y, HALF * z : HALF * z + 48, :] = piece
    second_copies = []
    for t in (2, 1, 3):
        y = lax.rem(tm + t, 4)
        p2a_s[y] = va[y, 0:A2].astype(BF16)
        copy = remote(
            p2a_s.at[y], p2a_r.at[t - 1], y2_ss.at[t - 1], y2_rs.at[t - 1], moved(tm=t)
        )
        copy.start()
        second_copies.append(copy)
    for copy in column_copies:
        copy.wait_recv()
    t_b[0:B1] = (
        vb[tm, 0:B1] + p1b_r[0].astype(F32) + p1b_r[1].astype(F32) + p1b_r[2].astype(F32)
    )
    for x in range(4):
        at = NB * HALF * x
        p2b_s[x] = t_b[at : at + B2].astype(BF16)
    for r in (2, 1, 3):
        x = lax.rem(row + r, 4)
        copy = remote(
            p2b_s.at[x], p2b_r.at[r - 1], x2_ss.at[r - 1], x2_rs.at[r - 1], moved(row=r)
        )
        copy.start()
        second_copies.append(copy)
    gs[2] = gain_sum(1, [1, 2, 3])
    for t in range(1, 4):
        gain_send(2, 3 + t, moved(tm=-t))
    for copy in second_copies[:3]:
        copy.wait_recv()
    u_a[0:A2] = va[tm, 0:A2] + p2a_r[0].astype(F32) + p2a_r[1].astype(F32) + p2a_r[2].astype(F32)
    for copy in second_copies[3:]:
        copy.wait_recv()
    mine = t_b[pl.ds(NB * HALF * row, B2), :]
    u_b[0:B2] = mine + p2b_r[0].astype(F32) + p2b_r[1].astype(F32) + p2b_r[2].astype(F32)
    gs[3] = gain_sum(2, [4, 5, 6])
    for d in range(1, 8):
        gain_send(3, 6 + d, moved(col=2 * d))
    for z in range(8):
        whole, at = (u_a, z) if z < NA else (u_b, z - NA)
        p3s[z] = whole[HALF * at : HALF * at + 48]
    depth_copies = []
    for d in range(1, 8):
        z = lax.rem(zed + d, 8)
        copy = remote(p3s.at[z], p3r.at[d - 1], z_ss.at[d - 1], z_rs.at[d - 1], moved(col=2 * d))
        copy.start()
        depth_copies.append(copy)
    total = p3s[zed]
    for d in range(7):
        depth_copies[d].wait_recv()
        total = total + p3r[d]
    wg_out[...] = total
    gg_out[...] = gain_sum(3, [7, 8, 9, 10, 11, 12, 13])

    for copy in tokens:
        copy.wait()
    for copy in halo + edges + first_rows + column_copies + second_copies:
        copy.wait_send()
    for copy in depth_copies + gain_copies:
        copy.wait_send()
    for chunk in range(len(PEER_CHUNKS)):
        for copy in peer_chunk(chunk):
            copy.wait_send()


def finish(ig_ref, wg_ref, gg_ref, ig_out, wg_out, gg_out):
    for f in range(2):
        wide = jnp.concatenate([ig_ref[f].astype(F32), jnp.zeros((256, 64), F32)], axis=1)
        ig_out[f] = jnp.transpose(wide)[:C].astype(BF16)
    square = jnp.concatenate([wg_ref[...], jnp.zeros((80, 128), F32)], axis=0)
    turned = jnp.transpose(square)
    wg_out[:, 0:41] = turned[0:48, 0:41]
    wg_out[:, 41:81] = turned[64:112, 0:40]
    gg_out[:, 0:128] = gg_ref[0:1]
    gg_out[:, 128:192] = gg_ref[1:2, 0:64]


def shards(features, norm_gain, conv_weight, out_grad):
    any_spec = pl.BlockSpec(memory_space=pl.ANY)
    vmem = pl.BlockSpec(memory_space=pltpu.VMEM)
    dma = pltpu.SemaphoreType.DMA
    scratch = [
        pltpu.VMEM((2, 16, 16, C), BF16),
        pltpu.VMEM((3, 4, 18, 16, C), BF16),
        pltpu.VMEM((C, 27 * C), BF16),
        pltpu.VMEM((27, C, C), BF16),
        pltpu.VMEM((2, 48, C), BF16),
        pltpu.VMEM((2, 2, 48, C), BF16),
        pltpu.VMEM((2, 48, C), F32),
        pltpu.VMEM((3, C, 512), BF16),
        pltpu.VMEM((3, 512, C), F32),
        pltpu.VMEM((5192, 128), F32),
        pltpu.VMEM((5192, 128), F32),
        pltpu.VMEM((5192, 128), F32),
        pltpu.VMEM((5192, 128), F32),
        pltpu.VMEM((4, A1, 128), F32),
        pltpu.VMEM((4, A1, 128), BF16),
        pltpu.VMEM((3, A1, 128), BF16),
        pltpu.VMEM((A1, 128), F32),
        pltpu.VMEM((4, B1_SCRATCH, 128), F32),
        pltpu.VMEM((4, B1, 128), BF16),
        pltpu.VMEM((3, B1, 128), BF16),
        pltpu.VMEM((B1_SCRATCH + 8, 128), F32),
        pltpu.VMEM((4, A2_SCRATCH, 128), F32),
        pltpu.VMEM((4, A2, 128), BF16),
        pltpu.VMEM((3, A2, 128), BF16),
        pltpu.VMEM((A2_SCRATCH, 128), F32),
        pltpu.VMEM((4, B2, 128), BF16),
        pltpu.VMEM((3, B2, 128), BF16),
        pltpu.VMEM((B2_SCRATCH, 128), F32),
        pltpu.VMEM((8, 48, 128), F32),
        pltpu.VMEM((7, 48, 128), F32),
        pltpu.VMEM((4, 8, 128), F32),
        pltpu.VMEM((14, 8, 128), F32),
        pltpu.VMEM((2, 16, 16, C), BF16),
        dma((3,)),
        dma((6,)), dma((6,)),
        dma((4,)), dma((4,)),
        dma((10,)), dma((10,)),
        dma((3,)), dma((3,)),
        dma((3,)), dma((3,)),
        dma((3,)), dma((3,)),
        dma((3,)), dma((3,)),
        dma((7,)), dma((7,)),
        dma((15,)), dma((15,)),
        dma((14,)), dma((14,)),
    ]
    ig, wg, gg = pl.pallas_call(
        kernel,
        out_shape=(
            jax.ShapeDtypeStruct((2, 256, C), BF16),
            jax.ShapeDtypeStruct((48, 128), F32),
            jax.ShapeDtypeStruct((8, 128), F32),
        ),
        in_specs=[any_spec, vmem, any_spec, any_spec],
        out_specs=(vmem, vmem, vmem),
        scratch_shapes=scratch,
        compiler_params=pltpu.CompilerParams(
            collective_id=0, has_side_effects=True, vmem_limit_bytes=56 * 2**20
        ),
        name="unit_backward",
    )(features, norm_gain.reshape(1, C), conv_weight.T, out_grad)
    ig, wg, gg = pl.pallas_call(
        finish,
        out_shape=(
            jax.ShapeDtypeStruct((2, C, 256), BF16),
            jax.ShapeDtypeStruct((48, 81), F32),
            jax.ShapeDtypeStruct((1, C), F32),
        ),
        in_specs=[vmem, vmem, vmem],
        out_specs=(vmem, vmem, vmem),
        name="finish",
    )(ig, wg, gg)
    return ig.transpose(0, 2, 1)[:, None], wg.T, gg.reshape(C)


def solution(mesh):
    in_specs = (P("tm", "row", "col", None), P(), P(), P("tm", "row", "col", None))
    out_specs = (P("tm", ("row", "col"), None, None), P(("row", "col"), "tm"), P())
    return jax.shard_map(shards, mesh=mesh, in_specs=in_specs, out_specs=out_specs, check_vma=False)
```

```python
import jax
import jax.numpy as jnp
from jax import lax
from jax.experimental import pallas as pl
from jax.experimental.pallas import tpu as pltpu
from jax.sharding import PartitionSpec as P

MESH = pl.DeviceIdType.MESH
AXES = ("tm", "row", "col")
SIZES = (4, 4, 16)
F32 = jnp.float32
BF16 = jnp.bfloat16
C = 192
EPS = 1e-06
NA = 3
NB = 8 - NA
HALF = 41


def tiles(rows, unit=16):
    return -(-rows // unit) * unit


LO = tiles(81 * (NA - 1) + 88)
HI = tiles(HALF * (NA - 1) + 48)
A1 = LO + HI
B1 = tiles(NB * HALF)
B1_SCRATCH = tiles(HALF * (NB - 1) + 48, 8)
A2 = tiles(NA * HALF)
A2_SCRATCH = tiles(HALF * (NA - 1) + 48, 8)
PEER_CHUNKS = ((22, 10), (11, 11), (8, 3), (4, 4), (0, 4))


def moved(tm=0, row=0, col=0):
    out = []
    for name, size, off in zip(AXES, SIZES, (tm, row, col)):
        out.append(lax.rem(lax.axis_index(name) + (off % size), size))
    return tuple(out)


REACHED = (
    [(-1, 0, 0), (-2, 0, 0), (-3, 0, 0)]
    + [(0, r, 0) for r in (1, 2, 3)]
    + [(-1, 1, 0), (-1, -1, 0), (-1, 0, 1), (-1, 0, -1)]
    + [(0, 0, d) for d in range(1, 16)]
)


def roll_w(x, forward):
    rows = x.shape[0]
    place = lax.rem(lax.broadcasted_iota(jnp.int32, x.shape, 0), 16)
    if forward:
        return jnp.where(place == 0, pltpu.roll(x, rows - 15, 0), pltpu.roll(x, 1, 0))
    return jnp.where(place == 15, pltpu.roll(x, 15, 0), pltpu.roll(x, rows - 1, 0))


def kernel(
    feat_hbm, gain_ref, w_hbm, grad_hbm,
    ig_out, wg_out, gg_out,
    f_v, gx, wt_v, w_v, e_s, e_r, e32, act_t, part, s_lo, s_hi, r_lo, r_hi,
    ffa, p1a_s, p1a_r, t_a, vb, p1b_s, p1b_r, t_b, va, p2a_s, p2a_r, u_a, p2b_s, p2b_r, u_b,
    p3s, p3r, gs, gr, ig,
    loc_sem, h_ss, h_rs, e_ss, e_rs, c_ss, c_rs, x_ss, x_rs, y_ss, y_rs, x2_ss, x2_rs, y2_ss, y2_rs, z_ss, z_rs,
    a_ss, a_rs, g_ss, g_rs,
):
    tm, row, col = (lax.axis_index(a) for a in AXES)
    core = lax.rem(col, 2)
    zed = col // 2
    peer = (tm, row, col + 1 - 2 * core)

    loads = [
        pltpu.make_async_copy(feat_hbm, f_v, loc_sem.at[0]),
        pltpu.make_async_copy(grad_hbm, gx.at[1, pl.ds(0, 2), pl.ds(1, 16)], loc_sem.at[1]),
        pltpu.make_async_copy(w_hbm, wt_v, loc_sem.at[2]),
    ]
    for load in loads:
        load.start()

    barrier = pltpu.get_barrier_semaphore()
    for off in REACHED:
        pl.semaphore_signal(
            barrier, inc=1, device_id=moved(*[-o for o in off]), device_id_type=MESH
        )
    pl.semaphore_wait(barrier, len(REACHED))

    def remote(src, dst, ss, rs, where):
        return pltpu.make_async_remote_copy(
            src_ref=src, dst_ref=dst, send_sem=ss, recv_sem=rs, device_id=where, device_id_type=MESH
        )

    halo = [
        remote(grad_hbm.at[:, 15], gx.at[1, pl.ds(0, 2), 0], h_ss.at[0], h_rs.at[0], moved(row=1)),
        remote(grad_hbm.at[:, 0], gx.at[1, pl.ds(0, 2), 17], h_ss.at[1], h_rs.at[1], moved(row=-1)),
        remote(grad_hbm.at[:, 15], gx.at[1, pl.ds(2, 2), 0], h_ss.at[2], h_rs.at[2], moved(tm=-1, row=1)),
        remote(grad_hbm.at[:, 0], gx.at[1, pl.ds(2, 2), 17], h_ss.at[3], h_rs.at[3], moved(tm=-1, row=-1)),
        remote(grad_hbm.at[0], gx.at[1, 2, pl.ds(1, 16)], h_ss.at[4], h_rs.at[4], moved(tm=-1)),
        remote(grad_hbm.at[1], gx.at[1, 3, pl.ds(1, 16)], h_ss.at[5], h_rs.at[5], moved(tm=-1)),
    ]
    for copy in halo:
        copy.start()

    gain = gain_ref[...]
    loads[0].wait()
    feat = f_v[...].reshape(512, C).astype(F32)
    scale = lax.rsqrt(jnp.mean(feat * feat, axis=-1, keepdims=True) + EPS)
    normed = feat * scale * gain
    act = normed * jax.nn.sigmoid(normed)
    act = act.astype(BF16).astype(F32)
    wide = jnp.concatenate([act, jnp.zeros((512, 64), F32)], axis=1)
    for kw in range(3):
        turned = wide if kw == 1 else roll_w(wide, kw == 0)
        act_t[kw] = jnp.transpose(turned)[:C].astype(BF16)

    def take_edges(dt):
        for side, edge in ((0, 0), (1, 15)):
            keep = col != edge
            if dt == 1:
                keep = jnp.logical_and(keep, tm != 3)
            e32[side] = jnp.where(keep, e_r[side, dt].astype(F32), 0.0)

    def insert_edges(s):
        place = lax.broadcasted_iota(jnp.int32, (16, C), 0)
        for h in range(18):
            n = 18 * (s % 2) + h
            mid = gx[1, s, h].astype(F32)
            left = jnp.broadcast_to(e32[0, n : n + 1, :], (16, C))
            right = jnp.broadcast_to(e32[1, n : n + 1, :], (16, C))
            gx[2, s, h] = jnp.where(place == 15, left, mid).astype(BF16)
            gx[0, s, h] = jnp.where(place == 0, right, mid).astype(BF16)

    def zero_unless(keep, s, h):
        gx[1, s, h] = jnp.where(keep, gx[1, s, h].astype(F32), 0.0).astype(BF16)

    loads[1].wait()
    halo[0].wait_recv()
    halo[1].wait_recv()
    for s in range(2):
        zero_unless(row != 0, s, 0)
        zero_unless(row != 3, s, 17)
    own = gx[1, pl.ds(0, 2)].reshape(576, C)
    for side, place in ((0, 15), (1, 0)):
        r = lax.broadcasted_iota(jnp.int32, (48, 576), 0)
        q = lax.broadcasted_iota(jnp.int32, (48, 576), 1)
        pick = jnp.where(jnp.logical_and(q == 16 * r + place, r < 36), 1.0, 0.0).astype(BF16)
        e_s[side] = jnp.dot(pick, own, preferred_element_type=F32).astype(BF16)
    edges = []
    for dt in range(2):
        for side, step in ((0, 1), (1, -1)):
            i = 2 * dt + side
            edges.append(
                remote(e_s.at[side], e_r.at[side, dt], e_ss.at[i], e_rs.at[i], moved(tm=-dt, col=step))
            )
    for copy in edges:
        copy.start()

    def cells_of(kt, kh, kw):
        return gx[kw, 2 - kt : 4 - kt, 2 - kh : 18 - kh].reshape(512, C)

    def weight_taps(kt, kh):
        for kw in range(3):
            k = 9 * kt + 3 * kh + kw
            wg = jnp.dot(act_t[kw], cells_of(kt, kh, kw), preferred_element_type=F32)
            s_lo[192 * k : 192 * k + 192, :] = wg[:, :128]
            s_hi[192 * k : 192 * k + 192, 0:64] = wg[:, 128:]

    def to_peer(chunk):
        def one(m, carry):
            start = pl.multiple_of((81 * (2 * m + 1 - core)) // 8 * 8, 8)
            rows = pl.ds(start, 88)
            for i, (src, dst) in enumerate(((s_lo, r_lo), (s_hi, r_hi))):
                sem = 2 * chunk + i
                remote(src.at[rows], dst.at[rows], c_ss.at[sem], c_rs.at[sem], peer).start()
            return carry

        first, count = PEER_CHUNKS[chunk]
        lax.fori_loop(first, first + count, one, 0)

    def peer_chunk(chunk):
        whole = pl.ds(0, PEER_CHUNKS[chunk][1] * 88)
        return [
            remote(src.at[whole], dst.at[whole], c_ss.at[2 * chunk + i], c_rs.at[2 * chunk + i], peer)
            for i, (src, dst) in enumerate(((s_lo, r_lo), (s_hi, r_hi)))
        ]

    lane = lax.broadcasted_iota(jnp.int32, (48, 128), 1)

    def slices(a, b, top, low):
        left = jnp.where(lane < 32, pltpu.roll(a, 32, 1), pltpu.roll(top, 32, 1))
        right = jnp.where(lane < 96, pltpu.roll(b, 96, 1), pltpu.roll(low, 96, 1))
        return (
            jnp.where(lane < 64, a, pltpu.roll(b, 64, 1)),
            jnp.where(lane < 64, pltpu.roll(a, 80, 1), pltpu.roll(b, 16, 1)),
            jnp.where(lane < 64, left, right),
            jnp.where(lane < 64, pltpu.roll(top, 112, 1), pltpu.roll(low, 48, 1)),
        )

    def gather(x):
        def both(own, other, start, rows):
            return own[pl.ds(start, rows), :] + other[pl.ds(start, rows), :]

        for z in range(8):
            start = 81 * (16 * x + 2 * z) + 81 * core
            top = both(s_hi, r_hi, start, 48)
            low = both(s_hi, r_hi, start + HALF, 48)
            if z < NA:
                ffa[x, 81 * z : 81 * z + 88, :] = both(s_lo, r_lo, start, 88)
                folded = jnp.where(lane < 64, top, pltpu.roll(low, 64, 1))
                ffa[x, LO + HALF * z : LO + HALF * z + 48, :] = folded
            else:
                a = both(s_lo, r_lo, start, 48)
                b = both(s_lo, r_lo, start + HALF, 48)
                at = HALF * (z - NA)
                for y, piece in enumerate(slices(a, b, top, low)):
                    vb[y, x, at : at + 48, :] = piece
        p1a_s[x] = ffa[x].astype(BF16)
        r = lax.rem(x + 4 - row, 4)

        @pl.when(r != 0)
        def _():
            remote(
                p1a_s.at[x], p1a_r.at[r - 1], x_ss.at[r - 1], x_rs.at[r - 1], (tm, x, col)
            ).start()

        for t in (2, 1, 3):
            y = lax.rem(tm + t, 4)
            p1b_s[y, x] = vb[y, x, 0:B1].astype(BF16)
            copy = first_columns(x, t)
            copy.start()

    def first_columns(x, t):
        y = lax.rem(tm + t, 4)
        i = 4 * (t - 1) + x
        return remote(
            p1b_s.at[y, x], p1b_r.at[t - 1, x], y_ss.at[i], y_rs.at[i], moved(tm=t)
        )

    def second_rows(x):
        total = vb[tm, x, 0:B1]
        for t in range(1, 4):
            first_columns(x, t).wait_recv()
            total = total + p1b_r[t - 1, x].astype(F32)
        t_b[x] = total
        p2b_s[x] = total.astype(BF16)
        r = lax.rem(x + 4 - row, 4)

        @pl.when(r != 0)
        def _():
            remote(
                p2b_s.at[x], p2b_r.at[r - 1], x2_ss.at[r - 1], x2_rs.at[r - 1], (tm, x, col)
            ).start()

    loads[2].wait()
    for k in range(27):
        w_v[k] = wt_v[:, 192 * k : 192 * k + 192]
    edges[0].wait_recv()
    edges[1].wait_recv()
    take_edges(0)
    insert_edges(0)
    insert_edges(1)
    for kh in range(3):
        weight_taps(2, kh)
    to_peer(0)

    edges[2].wait_recv()
    edges[3].wait_recv()
    take_edges(1)
    halo[2].wait_recv()
    halo[3].wait_recv()
    for s in (2, 3):
        halo[s + 2].wait_recv()
        zero_unless(row != 0, s, 0)
        zero_unless(row != 3, s, 17)

        @pl.when(tm == 3)
        def _(s=s):
            gx[1, s] = jnp.zeros((18, 16, C), BF16)

        insert_edges(s)
        if s == 2:
            for kh in range(3):
                weight_taps(1, kh)
            to_peer(1)
            for copy in peer_chunk(0):
                copy.wait_recv()
            gather(3)
        else:
            weight_taps(0, 2)
            to_peer(2)
            weight_taps(0, 1)
            to_peer(3)
            weight_taps(0, 0)
            to_peer(4)

    for copy in peer_chunk(1):
        copy.wait_recv()
    gather(2)
    for copy in peer_chunk(2):
        copy.wait_recv()
    gather(1)
    for chunk in (3, 4):
        for copy in peer_chunk(chunk):
            copy.wait_recv()
    gather(0)
    for kw in range(3):
        total = None
        for kt in range(3):
            for kh in range(3):
                more = jnp.dot(
                    cells_of(kt, kh, kw), w_v[9 * kt + 3 * kh + kw], preferred_element_type=F32
                )
                total = more if total is None else total + more
        part[kw] = total

    act_grad = part[1] + roll_w(part[2], True) + roll_w(part[0], False)
    feat = f_v[...].reshape(512, C).astype(F32)
    scale = lax.rsqrt(jnp.mean(feat * feat, axis=-1, keepdims=True) + EPS)
    unit = feat * scale
    normed = unit * gain
    sig = jax.nn.sigmoid(normed)
    normed_grad = act_grad * (sig * (1.0 + normed * (1.0 - sig)))
    gain_local = jnp.sum(normed_grad * unit, axis=0, keepdims=True)
    unit_grad = normed_grad * gain
    lean = jnp.mean(unit_grad * unit, axis=-1, keepdims=True)
    feat_grad = scale * (unit_grad - unit * lean)
    grad = gx[1, pl.ds(0, 2), pl.ds(1, 16)].reshape(512, C).astype(F32)
    ig[...] = (grad + feat_grad).astype(BF16).reshape(2, 16, 16, C)

    tokens = []
    for d in range(1, 16):
        there = lax.rem(col + d, 16)
        tokens.append(
            remote(
                ig.at[:, there],
                ig_out.at[:, pl.ds(pl.multiple_of(16 * col, 16), 16)],
                a_ss.at[d - 1],
                a_rs.at[d - 1],
                moved(col=d),
            )
        )
    for copy in tokens:
        copy.start()
    ig_out[:, pl.ds(pl.multiple_of(16 * col, 16), 16)] = ig[:, col]

    gs[0] = jnp.zeros((8, 128), F32)
    gs[0, pl.ds(0, 1), :] = gain_local[:, :128]
    gs[0, pl.ds(1, 1), pl.ds(0, 64)] = gain_local[:, 128:]
    gain_copies = []

    def gain_send(stage, slot, where):
        copy = remote(gs.at[stage], gr.at[slot], g_ss.at[slot], g_rs.at[slot], where)
        copy.start()
        gain_copies.append(copy)

    def gain_sum(stage, slots):
        total = gs[stage]
        for slot in slots:
            gain_copies[slot].wait_recv()
            total = total + gr[slot]
        return total

    gain_send(0, 0, peer)

    gs[1] = gain_sum(0, [0])
    for r in range(1, 4):
        gain_send(1, r, moved(row=r))

    second_rows(3)
    second_rows(2)
    first_rows = [
        remote(p1a_s.at[r], p1a_r.at[r - 1], x_ss.at[r - 1], x_rs.at[r - 1], moved(row=r))
        for r in (1, 2, 3)
    ]
    for copy in first_rows:
        copy.wait_recv()
    t_a[...] = ffa[row] + p1a_r[0].astype(F32) + p1a_r[1].astype(F32) + p1a_r[2].astype(F32)
    for z in range(NA):
        a = t_a[81 * z : 81 * z + 48, :]
        b = t_a[81 * z + HALF : 81 * z + HALF + 48, :]
        top = t_a[LO + HALF * z : LO + HALF * z + 48, :]
        for y, piece in enumerate(slices(a, b, top, pltpu.roll(top, 64, 1))):
            va[y, HALF * z : HALF * z + 48, :] = piece
    second_copies = []
    for t in (2, 1, 3):
        y = lax.rem(tm + t, 4)
        p2a_s[y] = va[y, 0:A2].astype(BF16)
        copy = remote(
            p2a_s.at[y], p2a_r.at[t - 1], y2_ss.at[t - 1], y2_rs.at[t - 1], moved(tm=t)
        )
        copy.start()
        second_copies.append(copy)
    second_rows(1)
    second_rows(0)
    gs[2] = gain_sum(1, [1, 2, 3])
    for t in range(1, 4):
        gain_send(2, 3 + t, moved(tm=-t))
    for copy in second_copies:
        copy.wait_recv()
    u_a[0:A2] = va[tm, 0:A2] + p2a_r[0].astype(F32) + p2a_r[1].astype(F32) + p2a_r[2].astype(F32)
    across = [
        remote(p2b_s.at[r], p2b_r.at[r - 1], x2_ss.at[r - 1], x2_rs.at[r - 1], moved(row=r))
        for r in (1, 2, 3)
    ]
    for copy in across:
        copy.wait_recv()
    u_b[0:B1] = t_b[row] + p2b_r[0].astype(F32) + p2b_r[1].astype(F32) + p2b_r[2].astype(F32)
    gs[3] = gain_sum(2, [4, 5, 6])
    for d in range(1, 8):
        gain_send(3, 6 + d, moved(col=2 * d))
    for z in range(8):
        whole, at = (u_a, z) if z < NA else (u_b, z - NA)
        p3s[z] = whole[HALF * at : HALF * at + 48]
    depth_copies = []
    for d in range(1, 8):
        z = lax.rem(zed + d, 8)
        copy = remote(p3s.at[z], p3r.at[d - 1], z_ss.at[d - 1], z_rs.at[d - 1], moved(col=2 * d))
        copy.start()
        depth_copies.append(copy)
    total = p3s[zed]
    for d in range(7):
        depth_copies[d].wait_recv()
        total = total + p3r[d]
    wg_out[...] = total
    gg_out[...] = gain_sum(3, [7, 8, 9, 10, 11, 12, 13])

    for copy in tokens:
        copy.wait()
    for copy in halo + edges + first_rows + second_copies + across:
        copy.wait_send()
    for copy in depth_copies + gain_copies:
        copy.wait_send()
    for x in range(4):
        for t in range(1, 4):
            first_columns(x, t).wait_send()
    for chunk in range(len(PEER_CHUNKS)):
        for copy in peer_chunk(chunk):
            copy.wait_send()


def finish(ig_ref, wg_ref, gg_ref, ig_out, wg_out, gg_out):
    for f in range(2):
        wide = jnp.concatenate([ig_ref[f].astype(F32), jnp.zeros((256, 64), F32)], axis=1)
        ig_out[f] = jnp.transpose(wide)[:C].astype(BF16)
    square = jnp.concatenate([wg_ref[...], jnp.zeros((80, 128), F32)], axis=0)
    turned = jnp.transpose(square)
    wg_out[:, 0:41] = turned[0:48, 0:41]
    wg_out[:, 41:81] = turned[64:112, 0:40]
    gg_out[:, 0:128] = gg_ref[0:1]
    gg_out[:, 128:192] = gg_ref[1:2, 0:64]


def shards(features, norm_gain, conv_weight, out_grad):
    any_spec = pl.BlockSpec(memory_space=pl.ANY)
    vmem = pl.BlockSpec(memory_space=pltpu.VMEM)
    dma = pltpu.SemaphoreType.DMA
    scratch = [
        pltpu.VMEM((2, 16, 16, C), BF16),
        pltpu.VMEM((3, 4, 18, 16, C), BF16),
        pltpu.VMEM((C, 27 * C), BF16),
        pltpu.VMEM((27, C, C), BF16),
        pltpu.VMEM((2, 48, C), BF16),
        pltpu.VMEM((2, 2, 48, C), BF16),
        pltpu.VMEM((2, 48, C), F32),
        pltpu.VMEM((3, C, 512), BF16),
        pltpu.VMEM((3, 512, C), F32),
        pltpu.VMEM((5192, 128), F32),
        pltpu.VMEM((5192, 128), F32),
        pltpu.VMEM((5192, 128), F32),
        pltpu.VMEM((5192, 128), F32),
        pltpu.VMEM((4, A1, 128), F32),
        pltpu.VMEM((4, A1, 128), BF16),
        pltpu.VMEM((3, A1, 128), BF16),
        pltpu.VMEM((A1, 128), F32),
        pltpu.VMEM((4, 4, B1_SCRATCH, 128), F32),
        pltpu.VMEM((4, 4, B1, 128), BF16),
        pltpu.VMEM((3, 4, B1, 128), BF16),
        pltpu.VMEM((4, B1, 128), F32),
        pltpu.VMEM((4, A2_SCRATCH, 128), F32),
        pltpu.VMEM((4, A2, 128), BF16),
        pltpu.VMEM((3, A2, 128), BF16),
        pltpu.VMEM((A2_SCRATCH, 128), F32),
        pltpu.VMEM((4, B1, 128), BF16),
        pltpu.VMEM((3, B1, 128), BF16),
        pltpu.VMEM((B1_SCRATCH, 128), F32),
        pltpu.VMEM((8, 48, 128), F32),
        pltpu.VMEM((7, 48, 128), F32),
        pltpu.VMEM((4, 8, 128), F32),
        pltpu.VMEM((14, 8, 128), F32),
        pltpu.VMEM((2, 16, 16, C), BF16),
        dma((3,)),
        dma((6,)), dma((6,)),
        dma((4,)), dma((4,)),
        dma((10,)), dma((10,)),
        dma((3,)), dma((3,)),
        dma((12,)), dma((12,)),
        dma((3,)), dma((3,)),
        dma((3,)), dma((3,)),
        dma((7,)), dma((7,)),
        dma((15,)), dma((15,)),
        dma((14,)), dma((14,)),
    ]
    ig, wg, gg = pl.pallas_call(
        kernel,
        out_shape=(
            jax.ShapeDtypeStruct((2, 256, C), BF16),
            jax.ShapeDtypeStruct((48, 128), F32),
            jax.ShapeDtypeStruct((8, 128), F32),
        ),
        in_specs=[any_spec, vmem, any_spec, any_spec],
        out_specs=(vmem, vmem, vmem),
        scratch_shapes=scratch,
        compiler_params=pltpu.CompilerParams(
            collective_id=0, has_side_effects=True, vmem_limit_bytes=56 * 2**20
        ),
        name="unit_backward",
    )(features, norm_gain.reshape(1, C), conv_weight.T, out_grad)
    ig, wg, gg = pl.pallas_call(
        finish,
        out_shape=(
            jax.ShapeDtypeStruct((2, C, 256), BF16),
            jax.ShapeDtypeStruct((48, 81), F32),
            jax.ShapeDtypeStruct((1, C), F32),
        ),
        in_specs=[vmem, vmem, vmem],
        out_specs=(vmem, vmem, vmem),
        name="finish",
    )(ig, wg, gg)
    return ig.transpose(0, 2, 1)[:, None], wg.T, gg.reshape(C)


def solution(mesh):
    in_specs = (P("tm", "row", "col", None), P(), P(), P("tm", "row", "col", None))
    out_specs = (P("tm", ("row", "col"), None, None), P(("row", "col"), "tm"), P())
    return jax.shard_map(shards, mesh=mesh, in_specs=in_specs, out_specs=out_specs, check_vma=False)
```

```python
import jax
import jax.numpy as jnp
from jax import lax
from jax.experimental import pallas as pl
from jax.experimental.pallas import tpu as pltpu
from jax.sharding import PartitionSpec as P

MESH = pl.DeviceIdType.MESH
AXES = ("tm", "row", "col")
SIZES = (4, 4, 16)
F32 = jnp.float32
BF16 = jnp.bfloat16
C = 192
EPS = 1e-06
NA = 3
NB = 8 - NA
HALF = 41


def tiles(rows, unit=16):
    return -(-rows // unit) * unit


LO = tiles(81 * (NA - 1) + 88)
HI = tiles(HALF * (NA - 1) + 48)
A1 = LO + HI
B1 = tiles(NB * HALF)
B1_SCRATCH = tiles(HALF * (NB - 1) + 48, 8)
A2 = tiles(NA * HALF)
A2_SCRATCH = tiles(HALF * (NA - 1) + 48, 8)
PEER_CHUNKS = ((22, 10), (11, 11), (8, 3), (4, 4), (0, 4))


def moved(tm=0, row=0, col=0):
    out = []
    for name, size, off in zip(AXES, SIZES, (tm, row, col)):
        out.append(lax.rem(lax.axis_index(name) + (off % size), size))
    return tuple(out)


REACHED = (
    [(-1, 0, 0), (-2, 0, 0), (-3, 0, 0)]
    + [(0, r, 0) for r in (1, 2, 3)]
    + [(-1, 1, 0), (-1, -1, 0), (-1, 0, 1), (-1, 0, -1)]
    + [(0, 0, d) for d in range(1, 16)]
)


def roll_w(x, forward):
    rows = x.shape[0]
    place = lax.rem(lax.broadcasted_iota(jnp.int32, x.shape, 0), 16)
    if forward:
        return jnp.where(place == 0, pltpu.roll(x, rows - 15, 0), pltpu.roll(x, 1, 0))
    return jnp.where(place == 15, pltpu.roll(x, 15, 0), pltpu.roll(x, rows - 1, 0))


def kernel(
    feat_hbm, gain_ref, w_hbm, grad_hbm,
    ig_out, wg_out, gg_out,
    f_v, gx, wt_v, w_v, e_s, e_r, e32, act_t, part, s_lo, s_hi, r_lo, r_hi,
    ffa, p1a_s, p1a_r, t_a, vb, p1b_s, p1b_r, t_b, va, p2a_s, p2a_r, u_a, p2b_s, p2b_r, u_b,
    p3s, p3r, gs, gr, ig,
    loc_sem, h_ss, h_rs, e_ss, e_rs, c_ss, c_rs, x_ss, x_rs, y_ss, y_rs, x2_ss, x2_rs, y2_ss, y2_rs, z_ss, z_rs,
    a_ss, a_rs, g_ss, g_rs,
):
    tm, row, col = (lax.axis_index(a) for a in AXES)
    core = lax.rem(col, 2)
    zed = col // 2
    peer = (tm, row, col + 1 - 2 * core)

    loads = [
        pltpu.make_async_copy(feat_hbm, f_v, loc_sem.at[0]),
        pltpu.make_async_copy(grad_hbm, gx.at[1, pl.ds(0, 2), pl.ds(1, 16)], loc_sem.at[1]),
        pltpu.make_async_copy(w_hbm, wt_v, loc_sem.at[2]),
    ]
    for load in loads:
        load.start()

    barrier = pltpu.get_barrier_semaphore()
    for off in REACHED:
        pl.semaphore_signal(
            barrier, inc=1, device_id=moved(*[-o for o in off]), device_id_type=MESH
        )
    pl.semaphore_wait(barrier, len(REACHED))

    def remote(src, dst, ss, rs, where):
        return pltpu.make_async_remote_copy(
            src_ref=src, dst_ref=dst, send_sem=ss, recv_sem=rs, device_id=where, device_id_type=MESH
        )

    halo = [
        remote(grad_hbm.at[:, 15], gx.at[1, pl.ds(0, 2), 0], h_ss.at[0], h_rs.at[0], moved(row=1)),
        remote(grad_hbm.at[:, 0], gx.at[1, pl.ds(0, 2), 17], h_ss.at[1], h_rs.at[1], moved(row=-1)),
        remote(grad_hbm.at[:, 15], gx.at[1, pl.ds(2, 2), 0], h_ss.at[2], h_rs.at[2], moved(tm=-1, row=1)),
        remote(grad_hbm.at[:, 0], gx.at[1, pl.ds(2, 2), 17], h_ss.at[3], h_rs.at[3], moved(tm=-1, row=-1)),
        remote(grad_hbm.at[0], gx.at[1, 2, pl.ds(1, 16)], h_ss.at[4], h_rs.at[4], moved(tm=-1)),
        remote(grad_hbm.at[1], gx.at[1, 3, pl.ds(1, 16)], h_ss.at[5], h_rs.at[5], moved(tm=-1)),
    ]
    for copy in halo:
        copy.start()

    gain = gain_ref[...]
    loads[0].wait()
    feat = f_v[...].reshape(512, C).astype(F32)
    scale = lax.rsqrt(jnp.mean(feat * feat, axis=-1, keepdims=True) + EPS)
    normed = feat * scale * gain
    act = normed * jax.nn.sigmoid(normed)
    act = act.astype(BF16).astype(F32)
    wide = jnp.concatenate([act, jnp.zeros((512, 64), F32)], axis=1)
    for kw in range(3):
        turned = wide if kw == 1 else roll_w(wide, kw == 0)
        act_t[kw] = jnp.transpose(turned)[:C].astype(BF16)

    def take_edges(dt):
        for side, edge in ((0, 0), (1, 15)):
            keep = col != edge
            if dt == 1:
                keep = jnp.logical_and(keep, tm != 3)
            e32[side] = jnp.where(keep, e_r[side, dt].astype(F32), 0.0)

    def insert_edges(s):
        place = lax.broadcasted_iota(jnp.int32, (16, C), 0)
        for h in range(18):
            n = 18 * (s % 2) + h
            mid = gx[1, s, h].astype(F32)
            left = jnp.broadcast_to(e32[0, n : n + 1, :], (16, C))
            right = jnp.broadcast_to(e32[1, n : n + 1, :], (16, C))
            gx[2, s, h] = jnp.where(place == 15, left, mid).astype(BF16)
            gx[0, s, h] = jnp.where(place == 0, right, mid).astype(BF16)

    def zero_unless(keep, s, h):
        gx[1, s, h] = jnp.where(keep, gx[1, s, h].astype(F32), 0.0).astype(BF16)

    loads[1].wait()
    halo[0].wait_recv()
    halo[1].wait_recv()
    for s in range(2):
        zero_unless(row != 0, s, 0)
        zero_unless(row != 3, s, 17)
    own = gx[1, pl.ds(0, 2)].reshape(576, C)
    for side, place in ((0, 15), (1, 0)):
        r = lax.broadcasted_iota(jnp.int32, (48, 576), 0)
        q = lax.broadcasted_iota(jnp.int32, (48, 576), 1)
        pick = jnp.where(jnp.logical_and(q == 16 * r + place, r < 36), 1.0, 0.0).astype(BF16)
        e_s[side] = jnp.dot(pick, own, preferred_element_type=F32).astype(BF16)
    edges = []
    for dt in range(2):
        for side, step in ((0, 1), (1, -1)):
            i = 2 * dt + side
            edges.append(
                remote(e_s.at[side], e_r.at[side, dt], e_ss.at[i], e_rs.at[i], moved(tm=-dt, col=step))
            )
    for copy in edges:
        copy.start()

    def cells_of(kt, kh, kw):
        return gx[kw, 2 - kt : 4 - kt, 2 - kh : 18 - kh].reshape(512, C)

    def weight_taps(kt, kh):
        for kw in range(3):
            k = 9 * kt + 3 * kh + kw
            wg = jnp.dot(act_t[kw], cells_of(kt, kh, kw), preferred_element_type=F32)
            s_lo[192 * k : 192 * k + 192, :] = wg[:, :128]
            s_hi[192 * k : 192 * k + 192, 0:64] = wg[:, 128:]

    def to_peer(chunk):
        def one(m, carry):
            start = pl.multiple_of((81 * (2 * m + 1 - core)) // 8 * 8, 8)
            rows = pl.ds(start, 88)
            for i, (src, dst) in enumerate(((s_lo, r_lo), (s_hi, r_hi))):
                sem = 2 * chunk + i
                remote(src.at[rows], dst.at[rows], c_ss.at[sem], c_rs.at[sem], peer).start()
            return carry

        first, count = PEER_CHUNKS[chunk]
        lax.fori_loop(first, first + count, one, 0)

    def peer_chunk(chunk):
        whole = pl.ds(0, PEER_CHUNKS[chunk][1] * 88)
        return [
            remote(src.at[whole], dst.at[whole], c_ss.at[2 * chunk + i], c_rs.at[2 * chunk + i], peer)
            for i, (src, dst) in enumerate(((s_lo, r_lo), (s_hi, r_hi)))
        ]

    lane = lax.broadcasted_iota(jnp.int32, (48, 128), 1)

    def slices(a, b, top, low):
        left = jnp.where(lane < 32, pltpu.roll(a, 32, 1), pltpu.roll(top, 32, 1))
        right = jnp.where(lane < 96, pltpu.roll(b, 96, 1), pltpu.roll(low, 96, 1))
        return (
            jnp.where(lane < 64, a, pltpu.roll(b, 64, 1)),
            jnp.where(lane < 64, pltpu.roll(a, 80, 1), pltpu.roll(b, 16, 1)),
            jnp.where(lane < 64, left, right),
            jnp.where(lane < 64, pltpu.roll(top, 112, 1), pltpu.roll(low, 48, 1)),
        )

    def gather(x):
        def both(own, other, start, rows):
            return own[pl.ds(start, rows), :] + other[pl.ds(start, rows), :]

        for z in range(8):
            start = 81 * (16 * x + 2 * z) + 81 * core
            top = both(s_hi, r_hi, start, 48)
            low = both(s_hi, r_hi, start + HALF, 48)
            if z < NA:
                ffa[x, 81 * z : 81 * z + 88, :] = both(s_lo, r_lo, start, 88)
                folded = jnp.where(lane < 64, top, pltpu.roll(low, 64, 1))
                ffa[x, LO + HALF * z : LO + HALF * z + 48, :] = folded
            else:
                a = both(s_lo, r_lo, start, 48)
                b = both(s_lo, r_lo, start + HALF, 48)
                at = HALF * (z - NA)
                for y, piece in enumerate(slices(a, b, top, low)):
                    vb[y, x, at : at + 48, :] = piece
        p1a_s[x] = ffa[x].astype(BF16)
        r = lax.rem(x + 4 - row, 4)

        @pl.when(r != 0)
        def _():
            remote(
                p1a_s.at[x], p1a_r.at[r - 1], x_ss.at[r - 1], x_rs.at[r - 1], (tm, x, col)
            ).start()

        for t in (2, 1, 3):
            y = lax.rem(tm + t, 4)
            p1b_s[y, x] = vb[y, x, 0:B1].astype(BF16)
            copy = first_columns(x, t)
            copy.start()

    def first_columns(x, t):
        y = lax.rem(tm + t, 4)
        i = 4 * (t - 1) + x
        return remote(
            p1b_s.at[y, x], p1b_r.at[t - 1, x], y_ss.at[i], y_rs.at[i], moved(tm=t)
        )

    def second_rows(x):
        total = vb[tm, x, 0:B1]
        for t in range(1, 4):
            first_columns(x, t).wait_recv()
            total = total + p1b_r[t - 1, x].astype(F32)
        t_b[x] = total
        p2b_s[x] = total.astype(BF16)
        r = lax.rem(x + 4 - row, 4)

        @pl.when(r != 0)
        def _():
            remote(
                p2b_s.at[x], p2b_r.at[r - 1], x2_ss.at[r - 1], x2_rs.at[r - 1], (tm, x, col)
            ).start()

    loads[2].wait()
    for k in range(27):
        w_v[k] = wt_v[:, 192 * k : 192 * k + 192]
    edges[0].wait_recv()
    edges[1].wait_recv()
    take_edges(0)
    insert_edges(0)
    insert_edges(1)
    for kh in range(3):
        weight_taps(2, kh)
    to_peer(0)

    edges[2].wait_recv()
    edges[3].wait_recv()
    take_edges(1)
    halo[2].wait_recv()
    halo[3].wait_recv()
    for s in (2, 3):
        halo[s + 2].wait_recv()
        zero_unless(row != 0, s, 0)
        zero_unless(row != 3, s, 17)

        @pl.when(tm == 3)
        def _(s=s):
            gx[1, s] = jnp.zeros((18, 16, C), BF16)

        insert_edges(s)
        if s == 2:
            for kh in range(3):
                weight_taps(1, kh)
            to_peer(1)
            for copy in peer_chunk(0):
                copy.wait_recv()
            gather(3)
        else:
            weight_taps(0, 2)
            to_peer(2)
            weight_taps(0, 1)
            to_peer(3)
            weight_taps(0, 0)
            to_peer(4)

    for copy in peer_chunk(1):
        copy.wait_recv()
    gather(2)
    for copy in peer_chunk(2):
        copy.wait_recv()
    gather(1)
    for chunk in (3, 4):
        for copy in peer_chunk(chunk):
            copy.wait_recv()
    gather(0)
    for kw in range(3):
        total = None
        for kt in range(3):
            for kh in range(3):
                more = jnp.dot(
                    cells_of(kt, kh, kw), w_v[9 * kt + 3 * kh + kw], preferred_element_type=F32
                )
                total = more if total is None else total + more
        part[kw] = total

    act_grad = part[1] + roll_w(part[2], True) + roll_w(part[0], False)
    feat = f_v[...].reshape(512, C).astype(F32)
    scale = lax.rsqrt(jnp.mean(feat * feat, axis=-1, keepdims=True) + EPS)
    unit = feat * scale
    normed = unit * gain
    sig = jax.nn.sigmoid(normed)
    normed_grad = act_grad * (sig * (1.0 + normed * (1.0 - sig)))
    gain_local = jnp.sum(normed_grad * unit, axis=0, keepdims=True)
    unit_grad = normed_grad * gain
    lean = jnp.mean(unit_grad * unit, axis=-1, keepdims=True)
    feat_grad = scale * (unit_grad - unit * lean)
    grad = gx[1, pl.ds(0, 2), pl.ds(1, 16)].reshape(512, C).astype(F32)
    ig[...] = (grad + feat_grad).astype(BF16).reshape(2, 16, 16, C)

    tokens = []
    for d in range(1, 16):
        there = lax.rem(col + d, 16)
        tokens.append(
            remote(
                ig.at[:, there],
                ig_out.at[:, pl.ds(pl.multiple_of(16 * col, 16), 16)],
                a_ss.at[d - 1],
                a_rs.at[d - 1],
                moved(col=d),
            )
        )
    for copy in tokens:
        copy.start()
    ig_out[:, pl.ds(pl.multiple_of(16 * col, 16), 16)] = ig[:, col]

    gs[0] = jnp.zeros((8, 128), F32)
    gs[0, pl.ds(0, 1), :] = gain_local[:, :128]
    gs[0, pl.ds(1, 1), pl.ds(0, 64)] = gain_local[:, 128:]
    gain_copies = []

    def gain_send(stage, slot, where):
        copy = remote(gs.at[stage], gr.at[slot], g_ss.at[slot], g_rs.at[slot], where)
        copy.start()
        gain_copies.append(copy)

    def gain_sum(stage, slots):
        total = gs[stage]
        for slot in slots:
            gain_copies[slot].wait_recv()
            total = total + gr[slot]
        return total

    gain_send(0, 0, peer)

    gs[1] = gain_sum(0, [0])
    for r in range(1, 4):
        gain_send(1, r, moved(row=r))

    second_rows(3)
    second_rows(2)
    first_rows = [
        remote(p1a_s.at[r], p1a_r.at[r - 1], x_ss.at[r - 1], x_rs.at[r - 1], moved(row=r))
        for r in (1, 2, 3)
    ]
    for copy in first_rows:
        copy.wait_recv()
    t_a[...] = ffa[row] + p1a_r[0].astype(F32) + p1a_r[1].astype(F32) + p1a_r[2].astype(F32)
    for z in range(NA):
        a = t_a[81 * z : 81 * z + 48, :]
        b = t_a[81 * z + HALF : 81 * z + HALF + 48, :]
        top = t_a[LO + HALF * z : LO + HALF * z + 48, :]
        for y, piece in enumerate(slices(a, b, top, pltpu.roll(top, 64, 1))):
            va[y, HALF * z : HALF * z + 48, :] = piece
    second_copies = []
    for t in (2, 1, 3):
        y = lax.rem(tm + t, 4)
        p2a_s[y] = va[y, 0:A2].astype(BF16)
        copy = remote(
            p2a_s.at[y], p2a_r.at[t - 1], y2_ss.at[t - 1], y2_rs.at[t - 1], moved(tm=t)
        )
        copy.start()
        second_copies.append(copy)
    second_rows(1)
    second_rows(0)
    gs[2] = gain_sum(1, [1, 2, 3])
    for t in range(1, 4):
        gain_send(2, 3 + t, moved(tm=-t))
    def depth(z, whole, at):
        p3s[z] = whole[HALF * at : HALF * at + 48]
        d = lax.rem(z + 8 - zed, 8)

        @pl.when(d != 0)
        def _():
            remote(
                p3s.at[z], p3r.at[d - 1], z_ss.at[d - 1], z_rs.at[d - 1],
                (tm, row, 2 * z + core),
            ).start()

    def a_part():
        for copy in second_copies:
            copy.wait_recv()
        u_a[0:A2] = (
            va[tm, 0:A2] + p2a_r[0].astype(F32) + p2a_r[1].astype(F32) + p2a_r[2].astype(F32)
        )
        for z in range(NA):
            depth(z, u_a, z)

    across = [
        remote(p2b_s.at[r], p2b_r.at[r - 1], x2_ss.at[r - 1], x2_rs.at[r - 1], moved(row=r))
        for r in (1, 2, 3)
    ]

    def b_part():
        for copy in across:
            copy.wait_recv()
        u_b[0:B1] = (
            t_b[row] + p2b_r[0].astype(F32) + p2b_r[1].astype(F32) + p2b_r[2].astype(F32)
        )
        for z in range(NA, 8):
            depth(z, u_b, z - NA)

    a_part()
    b_part()
    gs[3] = gain_sum(2, [4, 5, 6])
    for d in range(1, 8):
        gain_send(3, 6 + d, moved(col=2 * d))
    depth_copies = [
        remote(p3s.at[d], p3r.at[d - 1], z_ss.at[d - 1], z_rs.at[d - 1], moved(col=2 * d))
        for d in range(1, 8)
    ]
    total = p3s[zed]
    for d in range(7):
        depth_copies[d].wait_recv()
        total = total + p3r[d]
    wg_out[...] = total
    gg_out[...] = gain_sum(3, [7, 8, 9, 10, 11, 12, 13])

    for copy in tokens:
        copy.wait()
    for copy in halo + edges + first_rows + second_copies + across:
        copy.wait_send()
    for copy in depth_copies + gain_copies:
        copy.wait_send()
    for x in range(4):
        for t in range(1, 4):
            first_columns(x, t).wait_send()
    for chunk in range(len(PEER_CHUNKS)):
        for copy in peer_chunk(chunk):
            copy.wait_send()


def finish(ig_ref, wg_ref, gg_ref, ig_out, wg_out, gg_out):
    for f in range(2):
        wide = jnp.concatenate([ig_ref[f].astype(F32), jnp.zeros((256, 64), F32)], axis=1)
        ig_out[f] = jnp.transpose(wide)[:C].astype(BF16)
    square = jnp.concatenate([wg_ref[...], jnp.zeros((80, 128), F32)], axis=0)
    turned = jnp.transpose(square)
    wg_out[:, 0:41] = turned[0:48, 0:41]
    wg_out[:, 41:81] = turned[64:112, 0:40]
    gg_out[:, 0:128] = gg_ref[0:1]
    gg_out[:, 128:192] = gg_ref[1:2, 0:64]


def shards(features, norm_gain, conv_weight, out_grad):
    any_spec = pl.BlockSpec(memory_space=pl.ANY)
    vmem = pl.BlockSpec(memory_space=pltpu.VMEM)
    dma = pltpu.SemaphoreType.DMA
    scratch = [
        pltpu.VMEM((2, 16, 16, C), BF16),
        pltpu.VMEM((3, 4, 18, 16, C), BF16),
        pltpu.VMEM((C, 27 * C), BF16),
        pltpu.VMEM((27, C, C), BF16),
        pltpu.VMEM((2, 48, C), BF16),
        pltpu.VMEM((2, 2, 48, C), BF16),
        pltpu.VMEM((2, 48, C), F32),
        pltpu.VMEM((3, C, 512), BF16),
        pltpu.VMEM((3, 512, C), F32),
        pltpu.VMEM((5192, 128), F32),
        pltpu.VMEM((5192, 128), F32),
        pltpu.VMEM((5192, 128), F32),
        pltpu.VMEM((5192, 128), F32),
        pltpu.VMEM((4, A1, 128), F32),
        pltpu.VMEM((4, A1, 128), BF16),
        pltpu.VMEM((3, A1, 128), BF16),
        pltpu.VMEM((A1, 128), F32),
        pltpu.VMEM((4, 4, B1_SCRATCH, 128), F32),
        pltpu.VMEM((4, 4, B1, 128), BF16),
        pltpu.VMEM((3, 4, B1, 128), BF16),
        pltpu.VMEM((4, B1, 128), F32),
        pltpu.VMEM((4, A2_SCRATCH, 128), F32),
        pltpu.VMEM((4, A2, 128), BF16),
        pltpu.VMEM((3, A2, 128), BF16),
        pltpu.VMEM((A2_SCRATCH, 128), F32),
        pltpu.VMEM((4, B1, 128), BF16),
        pltpu.VMEM((3, B1, 128), BF16),
        pltpu.VMEM((B1_SCRATCH, 128), F32),
        pltpu.VMEM((8, 48, 128), F32),
        pltpu.VMEM((7, 48, 128), F32),
        pltpu.VMEM((4, 8, 128), F32),
        pltpu.VMEM((14, 8, 128), F32),
        pltpu.VMEM((2, 16, 16, C), BF16),
        dma((3,)),
        dma((6,)), dma((6,)),
        dma((4,)), dma((4,)),
        dma((10,)), dma((10,)),
        dma((3,)), dma((3,)),
        dma((12,)), dma((12,)),
        dma((3,)), dma((3,)),
        dma((3,)), dma((3,)),
        dma((7,)), dma((7,)),
        dma((15,)), dma((15,)),
        dma((14,)), dma((14,)),
    ]
    ig, wg, gg = pl.pallas_call(
        kernel,
        out_shape=(
            jax.ShapeDtypeStruct((2, 256, C), BF16),
            jax.ShapeDtypeStruct((48, 128), F32),
            jax.ShapeDtypeStruct((8, 128), F32),
        ),
        in_specs=[any_spec, vmem, any_spec, any_spec],
        out_specs=(vmem, vmem, vmem),
        scratch_shapes=scratch,
        compiler_params=pltpu.CompilerParams(
            collective_id=0, has_side_effects=True, vmem_limit_bytes=56 * 2**20
        ),
        name="unit_backward",
    )(features, norm_gain.reshape(1, C), conv_weight.T, out_grad)
    ig, wg, gg = pl.pallas_call(
        finish,
        out_shape=(
            jax.ShapeDtypeStruct((2, C, 256), BF16),
            jax.ShapeDtypeStruct((48, 81), F32),
            jax.ShapeDtypeStruct((1, C), F32),
        ),
        in_specs=[vmem, vmem, vmem],
        out_specs=(vmem, vmem, vmem),
        name="finish",
    )(ig, wg, gg)
    return ig.transpose(0, 2, 1)[:, None], wg.T, gg.reshape(C)


def solution(mesh):
    in_specs = (P("tm", "row", "col", None), P(), P(), P("tm", "row", "col", None))
    out_specs = (P("tm", ("row", "col"), None, None), P(("row", "col"), "tm"), P())
    return jax.shard_map(shards, mesh=mesh, in_specs=in_specs, out_specs=out_specs, check_vma=False)
```

```python
import jax
import jax.numpy as jnp
from jax import lax
from jax.experimental import pallas as pl
from jax.experimental.pallas import tpu as pltpu
from jax.sharding import PartitionSpec as P

MESH = pl.DeviceIdType.MESH
AXES = ("tm", "row", "col")
SIZES = (4, 4, 16)
F32 = jnp.float32
BF16 = jnp.bfloat16
C = 192
EPS = 1e-06
ZA = (0, 3, 6)
ZB = tuple(z for z in range(8) if z not in ZA)
NA, NB = len(ZA), len(ZB)
HALF = 41


def tiles(rows, unit=16):
    return -(-rows // unit) * unit


LO = tiles(81 * (NA - 1) + 88)
HI = tiles(HALF * (NA - 1) + 48)
A1 = LO + HI
B1 = tiles(NB * HALF)
B1_SCRATCH = tiles(HALF * (NB - 1) + 48, 8)
A2 = tiles(NA * HALF)
A2_SCRATCH = tiles(HALF * (NA - 1) + 48, 8)
PEER_CHUNKS = ((22, 10), (11, 11), (8, 3), (4, 4), (0, 4))


def moved(tm=0, row=0, col=0):
    out = []
    for name, size, off in zip(AXES, SIZES, (tm, row, col)):
        out.append(lax.rem(lax.axis_index(name) + (off % size), size))
    return tuple(out)


REACHED = (
    [(-1, 0, 0), (-2, 0, 0), (-3, 0, 0)]
    + [(0, r, 0) for r in (1, 2, 3)]
    + [(-1, 1, 0), (-1, -1, 0), (-1, 0, 1), (-1, 0, -1)]
    + [(0, 0, d) for d in range(1, 16)]
)


def roll_w(x, forward):
    rows = x.shape[0]
    place = lax.rem(lax.broadcasted_iota(jnp.int32, x.shape, 0), 16)
    if forward:
        return jnp.where(place == 0, pltpu.roll(x, rows - 15, 0), pltpu.roll(x, 1, 0))
    return jnp.where(place == 15, pltpu.roll(x, 15, 0), pltpu.roll(x, rows - 1, 0))


def kernel(
    feat_hbm, gain_ref, w_hbm, grad_hbm,
    ig_out, wg_out, gg_out,
    f_v, gx, wt_v, w_v, e_s, e_r, e32, act_t, part, s_lo, s_hi, r_lo, r_hi,
    ffa, p1a_s, p1a_r, t_a, vb, p1b_s, p1b_r, t_b, va, p2a_s, p2a_r, u_a, p2b_s, p2b_r, u_b,
    p3s, p3r, gs, gr, ig,
    loc_sem, h_ss, h_rs, e_ss, e_rs, c_ss, c_rs, x_ss, x_rs, y_ss, y_rs, x2_ss, x2_rs, y2_ss, y2_rs, z_ss, z_rs,
    a_ss, a_rs, g_ss, g_rs,
):
    tm, row, col = (lax.axis_index(a) for a in AXES)
    core = lax.rem(col, 2)
    zed = col // 2
    peer = (tm, row, col + 1 - 2 * core)

    loads = [
        pltpu.make_async_copy(feat_hbm, f_v, loc_sem.at[0]),
        pltpu.make_async_copy(grad_hbm, gx.at[1, pl.ds(0, 2), pl.ds(1, 16)], loc_sem.at[1]),
        pltpu.make_async_copy(w_hbm, wt_v, loc_sem.at[2]),
    ]
    for load in loads:
        load.start()

    barrier = pltpu.get_barrier_semaphore()
    for off in REACHED:
        pl.semaphore_signal(
            barrier, inc=1, device_id=moved(*[-o for o in off]), device_id_type=MESH
        )
    pl.semaphore_wait(barrier, len(REACHED))

    def remote(src, dst, ss, rs, where):
        return pltpu.make_async_remote_copy(
            src_ref=src, dst_ref=dst, send_sem=ss, recv_sem=rs, device_id=where, device_id_type=MESH
        )

    halo = [
        remote(grad_hbm.at[:, 15], gx.at[1, pl.ds(0, 2), 0], h_ss.at[0], h_rs.at[0], moved(row=1)),
        remote(grad_hbm.at[:, 0], gx.at[1, pl.ds(0, 2), 17], h_ss.at[1], h_rs.at[1], moved(row=-1)),
        remote(grad_hbm.at[:, 15], gx.at[1, pl.ds(2, 2), 0], h_ss.at[2], h_rs.at[2], moved(tm=-1, row=1)),
        remote(grad_hbm.at[:, 0], gx.at[1, pl.ds(2, 2), 17], h_ss.at[3], h_rs.at[3], moved(tm=-1, row=-1)),
        remote(grad_hbm.at[0], gx.at[1, 2, pl.ds(1, 16)], h_ss.at[4], h_rs.at[4], moved(tm=-1)),
        remote(grad_hbm.at[1], gx.at[1, 3, pl.ds(1, 16)], h_ss.at[5], h_rs.at[5], moved(tm=-1)),
    ]
    for copy in halo:
        copy.start()

    gain = gain_ref[...]
    loads[0].wait()
    feat = f_v[...].reshape(512, C).astype(F32)
    scale = lax.rsqrt(jnp.mean(feat * feat, axis=-1, keepdims=True) + EPS)
    normed = feat * scale * gain
    act = normed * jax.nn.sigmoid(normed)
    act = act.astype(BF16).astype(F32)
    wide = jnp.concatenate([act, jnp.zeros((512, 64), F32)], axis=1)
    for kw in range(3):
        turned = wide if kw == 1 else roll_w(wide, kw == 0)
        act_t[kw] = jnp.transpose(turned)[:C].astype(BF16)

    def take_edges(dt):
        for side, edge in ((0, 0), (1, 15)):
            keep = col != edge
            if dt == 1:
                keep = jnp.logical_and(keep, tm != 3)
            e32[side] = jnp.where(keep, e_r[side, dt].astype(F32), 0.0)

    def insert_edges(s):
        place = lax.broadcasted_iota(jnp.int32, (16, C), 0)
        for h in range(18):
            n = 18 * (s % 2) + h
            mid = gx[1, s, h].astype(F32)
            left = jnp.broadcast_to(e32[0, n : n + 1, :], (16, C))
            right = jnp.broadcast_to(e32[1, n : n + 1, :], (16, C))
            gx[2, s, h] = jnp.where(place == 15, left, mid).astype(BF16)
            gx[0, s, h] = jnp.where(place == 0, right, mid).astype(BF16)

    def zero_unless(keep, s, h):
        gx[1, s, h] = jnp.where(keep, gx[1, s, h].astype(F32), 0.0).astype(BF16)

    loads[1].wait()
    halo[0].wait_recv()
    halo[1].wait_recv()
    for s in range(2):
        zero_unless(row != 0, s, 0)
        zero_unless(row != 3, s, 17)
    own = gx[1, pl.ds(0, 2)].reshape(576, C)
    for side, place in ((0, 15), (1, 0)):
        r = lax.broadcasted_iota(jnp.int32, (48, 576), 0)
        q = lax.broadcasted_iota(jnp.int32, (48, 576), 1)
        pick = jnp.where(jnp.logical_and(q == 16 * r + place, r < 36), 1.0, 0.0).astype(BF16)
        e_s[side] = jnp.dot(pick, own, preferred_element_type=F32).astype(BF16)
    edges = []
    for dt in range(2):
        for side, step in ((0, 1), (1, -1)):
            i = 2 * dt + side
            edges.append(
                remote(e_s.at[side], e_r.at[side, dt], e_ss.at[i], e_rs.at[i], moved(tm=-dt, col=step))
            )
    for copy in edges:
        copy.start()

    def cells_of(kt, kh, kw):
        return gx[kw, 2 - kt : 4 - kt, 2 - kh : 18 - kh].reshape(512, C)

    def weight_taps(kt, kh):
        for kw in range(3):
            k = 9 * kt + 3 * kh + kw
            wg = jnp.dot(act_t[kw], cells_of(kt, kh, kw), preferred_element_type=F32)
            s_lo[192 * k : 192 * k + 192, :] = wg[:, :128]
            s_hi[192 * k : 192 * k + 192, 0:64] = wg[:, 128:]

    def to_peer(chunk):
        def one(m, carry):
            start = pl.multiple_of((81 * (2 * m + 1 - core)) // 8 * 8, 8)
            rows = pl.ds(start, 88)
            for i, (src, dst) in enumerate(((s_lo, r_lo), (s_hi, r_hi))):
                sem = 2 * chunk + i
                remote(src.at[rows], dst.at[rows], c_ss.at[sem], c_rs.at[sem], peer).start()
            return carry

        first, count = PEER_CHUNKS[chunk]
        lax.fori_loop(first, first + count, one, 0)

    def peer_chunk(chunk):
        whole = pl.ds(0, PEER_CHUNKS[chunk][1] * 88)
        return [
            remote(src.at[whole], dst.at[whole], c_ss.at[2 * chunk + i], c_rs.at[2 * chunk + i], peer)
            for i, (src, dst) in enumerate(((s_lo, r_lo), (s_hi, r_hi)))
        ]

    lane = lax.broadcasted_iota(jnp.int32, (48, 128), 1)

    def slices(a, b, top, low):
        left = jnp.where(lane < 32, pltpu.roll(a, 32, 1), pltpu.roll(top, 32, 1))
        right = jnp.where(lane < 96, pltpu.roll(b, 96, 1), pltpu.roll(low, 96, 1))
        return (
            jnp.where(lane < 64, a, pltpu.roll(b, 64, 1)),
            jnp.where(lane < 64, pltpu.roll(a, 80, 1), pltpu.roll(b, 16, 1)),
            jnp.where(lane < 64, left, right),
            jnp.where(lane < 64, pltpu.roll(top, 112, 1), pltpu.roll(low, 48, 1)),
        )

    def gather(x):
        def both(own, other, start, rows):
            return own[pl.ds(start, rows), :] + other[pl.ds(start, rows), :]

        for z in range(8):
            start = 81 * (16 * x + 2 * z) + 81 * core
            top = both(s_hi, r_hi, start, 48)
            low = both(s_hi, r_hi, start + HALF, 48)
            if z in ZA:
                i = ZA.index(z)
                ffa[x, 81 * i : 81 * i + 88, :] = both(s_lo, r_lo, start, 88)
                folded = jnp.where(lane < 64, top, pltpu.roll(low, 64, 1))
                ffa[x, LO + HALF * i : LO + HALF * i + 48, :] = folded
            else:
                a = both(s_lo, r_lo, start, 48)
                b = both(s_lo, r_lo, start + HALF, 48)
                at = HALF * ZB.index(z)
                for y, piece in enumerate(slices(a, b, top, low)):
                    vb[y, x, at : at + 48, :] = piece
        p1a_s[x] = ffa[x].astype(BF16)
        r = lax.rem(x + 4 - row, 4)

        @pl.when(r != 0)
        def _():
            remote(
                p1a_s.at[x], p1a_r.at[r - 1], x_ss.at[r - 1], x_rs.at[r - 1], (tm, x, col)
            ).start()

        for t in (2, 1, 3):
            y = lax.rem(tm + t, 4)
            p1b_s[y, x] = vb[y, x, 0:B1].astype(BF16)
            copy = first_columns(x, t)
            copy.start()

    def first_columns(x, t):
        y = lax.rem(tm + t, 4)
        i = 4 * (t - 1) + x
        return remote(
            p1b_s.at[y, x], p1b_r.at[t - 1, x], y_ss.at[i], y_rs.at[i], moved(tm=t)
        )

    def second_rows(x):
        total = vb[tm, x, 0:B1]
        for t in range(1, 4):
            first_columns(x, t).wait_recv()
            total = total + p1b_r[t - 1, x].astype(F32)
        t_b[x] = total
        p2b_s[x] = total.astype(BF16)
        r = lax.rem(x + 4 - row, 4)

        @pl.when(r != 0)
        def _():
            remote(
                p2b_s.at[x], p2b_r.at[r - 1], x2_ss.at[r - 1], x2_rs.at[r - 1], (tm, x, col)
            ).start()

    loads[2].wait()
    for k in range(27):
        w_v[k] = wt_v[:, 192 * k : 192 * k + 192]
    edges[0].wait_recv()
    edges[1].wait_recv()
    take_edges(0)
    insert_edges(0)
    insert_edges(1)
    for kh in range(3):
        weight_taps(2, kh)
    to_peer(0)

    edges[2].wait_recv()
    edges[3].wait_recv()
    take_edges(1)
    halo[2].wait_recv()
    halo[3].wait_recv()
    for s in (2, 3):
        halo[s + 2].wait_recv()
        zero_unless(row != 0, s, 0)
        zero_unless(row != 3, s, 17)

        @pl.when(tm == 3)
        def _(s=s):
            gx[1, s] = jnp.zeros((18, 16, C), BF16)

        insert_edges(s)
        if s == 2:
            for kh in range(3):
                weight_taps(1, kh)
            to_peer(1)
            for copy in peer_chunk(0):
                copy.wait_recv()
            gather(3)
        else:
            weight_taps(0, 2)
            to_peer(2)
            weight_taps(0, 1)
            to_peer(3)
            weight_taps(0, 0)
            to_peer(4)

    for copy in peer_chunk(1):
        copy.wait_recv()
    gather(2)
    for copy in peer_chunk(2):
        copy.wait_recv()
    gather(1)
    for chunk in (3, 4):
        for copy in peer_chunk(chunk):
            copy.wait_recv()
    gather(0)
    for kw in range(3):
        total = None
        for kt in range(3):
            for kh in range(3):
                more = jnp.dot(
                    cells_of(kt, kh, kw), w_v[9 * kt + 3 * kh + kw], preferred_element_type=F32
                )
                total = more if total is None else total + more
        part[kw] = total

    act_grad = part[1] + roll_w(part[2], True) + roll_w(part[0], False)
    feat = f_v[...].reshape(512, C).astype(F32)
    scale = lax.rsqrt(jnp.mean(feat * feat, axis=-1, keepdims=True) + EPS)
    unit = feat * scale
    normed = unit * gain
    sig = jax.nn.sigmoid(normed)
    normed_grad = act_grad * (sig * (1.0 + normed * (1.0 - sig)))
    gain_local = jnp.sum(normed_grad * unit, axis=0, keepdims=True)
    unit_grad = normed_grad * gain
    lean = jnp.mean(unit_grad * unit, axis=-1, keepdims=True)
    feat_grad = scale * (unit_grad - unit * lean)
    grad = gx[1, pl.ds(0, 2), pl.ds(1, 16)].reshape(512, C).astype(F32)
    ig[...] = (grad + feat_grad).astype(BF16).reshape(2, 16, 16, C)

    tokens = []
    for d in range(1, 16):
        there = lax.rem(col + d, 16)
        tokens.append(
            remote(
                ig.at[:, there],
                ig_out.at[:, pl.ds(pl.multiple_of(16 * col, 16), 16)],
                a_ss.at[d - 1],
                a_rs.at[d - 1],
                moved(col=d),
            )
        )
    for copy in tokens:
        copy.start()
    ig_out[:, pl.ds(pl.multiple_of(16 * col, 16), 16)] = ig[:, col]

    gs[0] = jnp.zeros((8, 128), F32)
    gs[0, pl.ds(0, 1), :] = gain_local[:, :128]
    gs[0, pl.ds(1, 1), pl.ds(0, 64)] = gain_local[:, 128:]
    gain_copies = []

    def gain_send(stage, slot, where):
        copy = remote(gs.at[stage], gr.at[slot], g_ss.at[slot], g_rs.at[slot], where)
        copy.start()
        gain_copies.append(copy)

    def gain_sum(stage, slots):
        total = gs[stage]
        for slot in slots:
            gain_copies[slot].wait_recv()
            total = total + gr[slot]
        return total

    gain_send(0, 0, peer)

    gs[1] = gain_sum(0, [0])
    for r in range(1, 4):
        gain_send(1, r, moved(row=r))

    second_rows(3)
    second_rows(2)
    first_rows = [
        remote(p1a_s.at[r], p1a_r.at[r - 1], x_ss.at[r - 1], x_rs.at[r - 1], moved(row=r))
        for r in (1, 2, 3)
    ]
    for copy in first_rows:
        copy.wait_recv()
    t_a[...] = ffa[row] + p1a_r[0].astype(F32) + p1a_r[1].astype(F32) + p1a_r[2].astype(F32)
    for z in range(NA):
        a = t_a[81 * z : 81 * z + 48, :]
        b = t_a[81 * z + HALF : 81 * z + HALF + 48, :]
        top = t_a[LO + HALF * z : LO + HALF * z + 48, :]
        for y, piece in enumerate(slices(a, b, top, pltpu.roll(top, 64, 1))):
            va[y, HALF * z : HALF * z + 48, :] = piece
    second_copies = []
    for t in (2, 1, 3):
        y = lax.rem(tm + t, 4)
        p2a_s[y] = va[y, 0:A2].astype(BF16)
        copy = remote(
            p2a_s.at[y], p2a_r.at[t - 1], y2_ss.at[t - 1], y2_rs.at[t - 1], moved(tm=t)
        )
        copy.start()
        second_copies.append(copy)
    second_rows(1)
    second_rows(0)
    gs[2] = gain_sum(1, [1, 2, 3])
    for t in range(1, 4):
        gain_send(2, 3 + t, moved(tm=-t))
    def depth(z, whole, at):
        p3s[z] = whole[HALF * at : HALF * at + 48]
        d = lax.rem(z + 8 - zed, 8)

        @pl.when(d != 0)
        def _():
            remote(
                p3s.at[z], p3r.at[d - 1], z_ss.at[d - 1], z_rs.at[d - 1],
                (tm, row, 2 * z + core),
            ).start()

    def a_part():
        for copy in second_copies:
            copy.wait_recv()
        u_a[0:A2] = (
            va[tm, 0:A2] + p2a_r[0].astype(F32) + p2a_r[1].astype(F32) + p2a_r[2].astype(F32)
        )
        for i, z in enumerate(ZA):
            depth(z, u_a, i)

    across = [
        remote(p2b_s.at[r], p2b_r.at[r - 1], x2_ss.at[r - 1], x2_rs.at[r - 1], moved(row=r))
        for r in (1, 2, 3)
    ]

    def b_part():
        for copy in across:
            copy.wait_recv()
        u_b[0:B1] = (
            t_b[row] + p2b_r[0].astype(F32) + p2b_r[1].astype(F32) + p2b_r[2].astype(F32)
        )
        for i, z in enumerate(ZB):
            depth(z, u_b, i)

    a_part()
    gs[3] = gain_sum(2, [4, 5, 6])
    for d in range(1, 8):
        gain_send(3, 6 + d, moved(col=2 * d))
    b_part()
    depth_copies = [
        remote(p3s.at[d], p3r.at[d - 1], z_ss.at[d - 1], z_rs.at[d - 1], moved(col=2 * d))
        for d in range(1, 8)
    ]
    total = p3s[zed]
    for d in range(7):
        depth_copies[d].wait_recv()
        total = total + p3r[d]
    wg_out[...] = total
    gg_out[...] = gain_sum(3, [7, 8, 9, 10, 11, 12, 13])

    for copy in tokens:
        copy.wait()
    for copy in halo + edges + first_rows + second_copies + across:
        copy.wait_send()
    for copy in depth_copies + gain_copies:
        copy.wait_send()
    for x in range(4):
        for t in range(1, 4):
            first_columns(x, t).wait_send()
    for chunk in range(len(PEER_CHUNKS)):
        for copy in peer_chunk(chunk):
            copy.wait_send()


def finish(ig_ref, wg_ref, gg_ref, ig_out, wg_out, gg_out):
    for f in range(2):
        wide = jnp.concatenate([ig_ref[f].astype(F32), jnp.zeros((256, 64), F32)], axis=1)
        ig_out[f] = jnp.transpose(wide)[:C].astype(BF16)
    square = jnp.concatenate([wg_ref[...], jnp.zeros((80, 128), F32)], axis=0)
    turned = jnp.transpose(square)
    wg_out[:, 0:41] = turned[0:48, 0:41]
    wg_out[:, 41:81] = turned[64:112, 0:40]
    gg_out[:, 0:128] = gg_ref[0:1]
    gg_out[:, 128:192] = gg_ref[1:2, 0:64]


def shards(features, norm_gain, conv_weight, out_grad):
    any_spec = pl.BlockSpec(memory_space=pl.ANY)
    vmem = pl.BlockSpec(memory_space=pltpu.VMEM)
    dma = pltpu.SemaphoreType.DMA
    scratch = [
        pltpu.VMEM((2, 16, 16, C), BF16),
        pltpu.VMEM((3, 4, 18, 16, C), BF16),
        pltpu.VMEM((C, 27 * C), BF16),
        pltpu.VMEM((27, C, C), BF16),
        pltpu.VMEM((2, 48, C), BF16),
        pltpu.VMEM((2, 2, 48, C), BF16),
        pltpu.VMEM((2, 48, C), F32),
        pltpu.VMEM((3, C, 512), BF16),
        pltpu.VMEM((3, 512, C), F32),
        pltpu.VMEM((5192, 128), F32),
        pltpu.VMEM((5192, 128), F32),
        pltpu.VMEM((5192, 128), F32),
        pltpu.VMEM((5192, 128), F32),
        pltpu.VMEM((4, A1, 128), F32),
        pltpu.VMEM((4, A1, 128), BF16),
        pltpu.VMEM((3, A1, 128), BF16),
        pltpu.VMEM((A1, 128), F32),
        pltpu.VMEM((4, 4, B1_SCRATCH, 128), F32),
        pltpu.VMEM((4, 4, B1, 128), BF16),
        pltpu.VMEM((3, 4, B1, 128), BF16),
        pltpu.VMEM((4, B1, 128), F32),
        pltpu.VMEM((4, A2_SCRATCH, 128), F32),
        pltpu.VMEM((4, A2, 128), BF16),
        pltpu.VMEM((3, A2, 128), BF16),
        pltpu.VMEM((A2_SCRATCH, 128), F32),
        pltpu.VMEM((4, B1, 128), BF16),
        pltpu.VMEM((3, B1, 128), BF16),
        pltpu.VMEM((B1_SCRATCH, 128), F32),
        pltpu.VMEM((8, 48, 128), F32),
        pltpu.VMEM((7, 48, 128), F32),
        pltpu.VMEM((4, 8, 128), F32),
        pltpu.VMEM((14, 8, 128), F32),
        pltpu.VMEM((2, 16, 16, C), BF16),
        dma((3,)),
        dma((6,)), dma((6,)),
        dma((4,)), dma((4,)),
        dma((10,)), dma((10,)),
        dma((3,)), dma((3,)),
        dma((12,)), dma((12,)),
        dma((3,)), dma((3,)),
        dma((3,)), dma((3,)),
        dma((7,)), dma((7,)),
        dma((15,)), dma((15,)),
        dma((14,)), dma((14,)),
    ]
    ig, wg, gg = pl.pallas_call(
        kernel,
        out_shape=(
            jax.ShapeDtypeStruct((2, 256, C), BF16),
            jax.ShapeDtypeStruct((48, 128), F32),
            jax.ShapeDtypeStruct((8, 128), F32),
        ),
        in_specs=[any_spec, vmem, any_spec, any_spec],
        out_specs=(vmem, vmem, vmem),
        scratch_shapes=scratch,
        compiler_params=pltpu.CompilerParams(
            collective_id=0, has_side_effects=True, vmem_limit_bytes=56 * 2**20
        ),
        name="unit_backward",
    )(features, norm_gain.reshape(1, C), conv_weight.T, out_grad)
    ig, wg, gg = pl.pallas_call(
        finish,
        out_shape=(
            jax.ShapeDtypeStruct((2, C, 256), BF16),
            jax.ShapeDtypeStruct((48, 81), F32),
            jax.ShapeDtypeStruct((1, C), F32),
        ),
        in_specs=[vmem, vmem, vmem],
        out_specs=(vmem, vmem, vmem),
        name="finish",
    )(ig, wg, gg)
    return ig.transpose(0, 2, 1)[:, None], wg.T, gg.reshape(C)


def solution(mesh):
    in_specs = (P("tm", "row", "col", None), P(), P(), P("tm", "row", "col", None))
    out_specs = (P("tm", ("row", "col"), None, None), P(("row", "col"), "tm"), P())
    return jax.shard_map(shards, mesh=mesh, in_specs=in_specs, out_specs=out_specs, check_vma=False)
```

```python
import jax
import jax.numpy as jnp
from jax import lax
from jax.experimental import pallas as pl
from jax.experimental.pallas import tpu as pltpu
from jax.sharding import PartitionSpec as P

MESH = pl.DeviceIdType.MESH
AXES = ("tm", "row", "col")
SIZES = (4, 4, 16)
F32 = jnp.float32
BF16 = jnp.bfloat16
C = 192
EPS = 1e-06
ZA = (0, 3, 6)
ZB = tuple(z for z in range(8) if z not in ZA)
NA, NB = len(ZA), len(ZB)
HALF = 41


def tiles(rows, unit=16):
    return -(-rows // unit) * unit


LO = tiles(81 * (NA - 1) + 88)
HI = tiles(HALF * (NA - 1) + 48)
A1 = LO + HI
B1 = tiles(NB * HALF)
B1_SCRATCH = tiles(HALF * (NB - 1) + 48, 8)
A2 = tiles(NA * HALF)
A2_SCRATCH = tiles(HALF * (NA - 1) + 48, 8)
PEER_CHUNKS = ((22, 10), (11, 11), (8, 3), (4, 4), (0, 4))


def moved(tm=0, row=0, col=0):
    out = []
    for name, size, off in zip(AXES, SIZES, (tm, row, col)):
        out.append(lax.rem(lax.axis_index(name) + (off % size), size))
    return tuple(out)


REACHED = (
    [(-1, 0, 0), (-2, 0, 0), (-3, 0, 0)]
    + [(0, r, 0) for r in (1, 2, 3)]
    + [(-1, 1, 0), (-1, -1, 0), (-1, 0, 1), (-1, 0, -1)]
    + [(0, 0, d) for d in range(1, 16)]
)


def roll_w(x, forward):
    rows = x.shape[0]
    place = lax.rem(lax.broadcasted_iota(jnp.int32, x.shape, 0), 16)
    if forward:
        return jnp.where(place == 0, pltpu.roll(x, rows - 15, 0), pltpu.roll(x, 1, 0))
    return jnp.where(place == 15, pltpu.roll(x, 15, 0), pltpu.roll(x, rows - 1, 0))


def kernel(
    feat_hbm, gain_ref, w_hbm, grad_hbm,
    ig_out, wg_out, gg_out,
    f_v, gx, wt_v, w_v, e_s, e_r, e32, act_t, part, s_lo, s_hi, r_lo, r_hi,
    ffa, p1a_s, p1a_r, t_a, vb, p1b_s, p1b_r, t_b, va, p2a_s, p2a_r, u_a, p2b_s, p2b_r, u_b,
    p3s, p3r, gs, gr, ig,
    loc_sem, h_ss, h_rs, e_ss, e_rs, c_ss, c_rs, x_ss, x_rs, y_ss, y_rs, x2_ss, x2_rs, y2_ss, y2_rs, z_ss, z_rs,
    a_ss, a_rs, g_ss, g_rs,
):
    tm, row, col = (lax.axis_index(a) for a in AXES)
    core = lax.rem(col, 2)
    zed = col // 2
    peer = (tm, row, col + 1 - 2 * core)

    loads = [
        pltpu.make_async_copy(feat_hbm, f_v, loc_sem.at[0]),
        pltpu.make_async_copy(grad_hbm, gx.at[1, pl.ds(0, 2), pl.ds(1, 16)], loc_sem.at[1]),
        pltpu.make_async_copy(w_hbm, wt_v, loc_sem.at[2]),
    ]
    for load in loads:
        load.start()

    barrier = pltpu.get_barrier_semaphore()
    for off in REACHED:
        pl.semaphore_signal(
            barrier, inc=1, device_id=moved(*[-o for o in off]), device_id_type=MESH
        )
    pl.semaphore_wait(barrier, len(REACHED))

    def remote(src, dst, ss, rs, where):
        return pltpu.make_async_remote_copy(
            src_ref=src, dst_ref=dst, send_sem=ss, recv_sem=rs, device_id=where, device_id_type=MESH
        )

    halo = [
        remote(grad_hbm.at[:, 15], gx.at[1, pl.ds(0, 2), 0], h_ss.at[0], h_rs.at[0], moved(row=1)),
        remote(grad_hbm.at[:, 0], gx.at[1, pl.ds(0, 2), 17], h_ss.at[1], h_rs.at[1], moved(row=-1)),
        remote(grad_hbm.at[:, 15], gx.at[1, pl.ds(2, 2), 0], h_ss.at[2], h_rs.at[2], moved(tm=-1, row=1)),
        remote(grad_hbm.at[:, 0], gx.at[1, pl.ds(2, 2), 17], h_ss.at[3], h_rs.at[3], moved(tm=-1, row=-1)),
        remote(grad_hbm.at[0], gx.at[1, 2, pl.ds(1, 16)], h_ss.at[4], h_rs.at[4], moved(tm=-1)),
        remote(grad_hbm.at[1], gx.at[1, 3, pl.ds(1, 16)], h_ss.at[5], h_rs.at[5], moved(tm=-1)),
    ]
    for copy in halo:
        copy.start()

    gain = gain_ref[...]
    loads[0].wait()
    feat = f_v[...].reshape(512, C).astype(F32)
    scale = lax.rsqrt(jnp.mean(feat * feat, axis=-1, keepdims=True) + EPS)
    normed = feat * scale * gain
    act = normed * jax.nn.sigmoid(normed)
    act = act.astype(BF16).astype(F32)
    wide = jnp.concatenate([act, jnp.zeros((512, 64), F32)], axis=1)
    for kw in range(3):
        turned = wide if kw == 1 else roll_w(wide, kw == 0)
        act_t[kw] = jnp.transpose(turned)[:C].astype(BF16)

    def take_edges(dt):
        for side, edge in ((0, 0), (1, 15)):
            keep = col != edge
            if dt == 1:
                keep = jnp.logical_and(keep, tm != 3)
            e32[side] = jnp.where(keep, e_r[side, dt].astype(F32), 0.0)

    def insert_edges(s):
        place = lax.broadcasted_iota(jnp.int32, (16, C), 0)
        for h in range(18):
            n = 18 * (s % 2) + h
            mid = gx[1, s, h].astype(F32)
            left = jnp.broadcast_to(e32[0, n : n + 1, :], (16, C))
            right = jnp.broadcast_to(e32[1, n : n + 1, :], (16, C))
            gx[2, s, h] = jnp.where(place == 15, left, mid).astype(BF16)
            gx[0, s, h] = jnp.where(place == 0, right, mid).astype(BF16)

    def zero_unless(keep, s, h):
        gx[1, s, h] = jnp.where(keep, gx[1, s, h].astype(F32), 0.0).astype(BF16)

    loads[1].wait()
    halo[0].wait_recv()
    halo[1].wait_recv()
    for s in range(2):
        zero_unless(row != 0, s, 0)
        zero_unless(row != 3, s, 17)
    own = gx[1, pl.ds(0, 2)].reshape(576, C)
    for side, place in ((0, 15), (1, 0)):
        r = lax.broadcasted_iota(jnp.int32, (48, 576), 0)
        q = lax.broadcasted_iota(jnp.int32, (48, 576), 1)
        pick = jnp.where(jnp.logical_and(q == 16 * r + place, r < 36), 1.0, 0.0).astype(BF16)
        e_s[side] = jnp.dot(pick, own, preferred_element_type=F32).astype(BF16)
    edges = []
    for dt in range(2):
        for side, step in ((0, 1), (1, -1)):
            i = 2 * dt + side
            edges.append(
                remote(e_s.at[side], e_r.at[side, dt], e_ss.at[i], e_rs.at[i], moved(tm=-dt, col=step))
            )
    for copy in edges:
        copy.start()

    def cells_of(kt, kh, kw):
        return gx[kw, 2 - kt : 4 - kt, 2 - kh : 18 - kh].reshape(512, C)

    def weight_taps(kt, kh):
        for kw in range(3):
            k = 9 * kt + 3 * kh + kw
            wg = jnp.dot(act_t[kw], cells_of(kt, kh, kw), preferred_element_type=F32)
            s_lo[192 * k : 192 * k + 192, :] = wg[:, :128]
            s_hi[192 * k : 192 * k + 192, 0:64] = wg[:, 128:]

    def to_peer(chunk):
        def one(m, carry):
            start = pl.multiple_of((81 * (2 * m + 1 - core)) // 8 * 8, 8)
            rows = pl.ds(start, 88)
            for i, (src, dst) in enumerate(((s_lo, r_lo), (s_hi, r_hi))):
                sem = 2 * chunk + i
                remote(src.at[rows], dst.at[rows], c_ss.at[sem], c_rs.at[sem], peer).start()
            return carry

        first, count = PEER_CHUNKS[chunk]
        lax.fori_loop(first, first + count, one, 0)

    def peer_chunk(chunk):
        whole = pl.ds(0, PEER_CHUNKS[chunk][1] * 88)
        return [
            remote(src.at[whole], dst.at[whole], c_ss.at[2 * chunk + i], c_rs.at[2 * chunk + i], peer)
            for i, (src, dst) in enumerate(((s_lo, r_lo), (s_hi, r_hi)))
        ]

    lane = lax.broadcasted_iota(jnp.int32, (48, 128), 1)

    def slices(a, b, top, low):
        left = jnp.where(lane < 32, pltpu.roll(a, 32, 1), pltpu.roll(top, 32, 1))
        right = jnp.where(lane < 96, pltpu.roll(b, 96, 1), pltpu.roll(low, 96, 1))
        return (
            jnp.where(lane < 64, a, pltpu.roll(b, 64, 1)),
            jnp.where(lane < 64, pltpu.roll(a, 80, 1), pltpu.roll(b, 16, 1)),
            jnp.where(lane < 64, left, right),
            jnp.where(lane < 64, pltpu.roll(top, 112, 1), pltpu.roll(low, 48, 1)),
        )

    def gather(x):
        def both(own, other, start, rows):
            return own[pl.ds(start, rows), :] + other[pl.ds(start, rows), :]

        for z in range(8):
            start = 81 * (16 * x + 2 * z) + 81 * core
            top = both(s_hi, r_hi, start, 48)
            low = both(s_hi, r_hi, start + HALF, 48)
            if z in ZA:
                i = ZA.index(z)
                ffa[x, 81 * i : 81 * i + 88, :] = both(s_lo, r_lo, start, 88)
                folded = jnp.where(lane < 64, top, pltpu.roll(low, 64, 1))
                ffa[x, LO + HALF * i : LO + HALF * i + 48, :] = folded
            else:
                a = both(s_lo, r_lo, start, 48)
                b = both(s_lo, r_lo, start + HALF, 48)
                at = HALF * ZB.index(z)
                for y, piece in enumerate(slices(a, b, top, low)):
                    vb[y, x, at : at + 48, :] = piece
        p1a_s[x] = ffa[x].astype(BF16)
        r = lax.rem(x + 4 - row, 4)

        @pl.when(r != 0)
        def _():
            remote(
                p1a_s.at[x], p1a_r.at[r - 1], x_ss.at[r - 1], x_rs.at[r - 1], (tm, x, col)
            ).start()

        for t in (2, 1, 3):
            y = lax.rem(tm + t, 4)
            p1b_s[y, x] = vb[y, x, 0:B1].astype(BF16)
            copy = first_columns(x, t)
            copy.start()

    def first_columns(x, t):
        y = lax.rem(tm + t, 4)
        i = 4 * (t - 1) + x
        return remote(
            p1b_s.at[y, x], p1b_r.at[t - 1, x], y_ss.at[i], y_rs.at[i], moved(tm=t)
        )

    def second_rows(x):
        total = vb[tm, x, 0:B1]
        for t in range(1, 4):
            first_columns(x, t).wait_recv()
            total = total + p1b_r[t - 1, x].astype(F32)
        t_b[x] = total
        p2b_s[x] = total.astype(BF16)
        r = lax.rem(x + 4 - row, 4)

        @pl.when(r != 0)
        def _():
            remote(
                p2b_s.at[x], p2b_r.at[r - 1], x2_ss.at[r - 1], x2_rs.at[r - 1], (tm, x, col)
            ).start()

    loads[2].wait()
    for k in range(27):
        w_v[k] = wt_v[:, 192 * k : 192 * k + 192]
    edges[0].wait_recv()
    edges[1].wait_recv()
    take_edges(0)
    insert_edges(0)
    insert_edges(1)
    for kh in range(3):
        weight_taps(2, kh)
    to_peer(0)

    edges[2].wait_recv()
    edges[3].wait_recv()
    take_edges(1)
    halo[2].wait_recv()
    halo[3].wait_recv()
    for s in (2, 3):
        halo[s + 2].wait_recv()
        zero_unless(row != 0, s, 0)
        zero_unless(row != 3, s, 17)

        @pl.when(tm == 3)
        def _(s=s):
            gx[1, s] = jnp.zeros((18, 16, C), BF16)

        insert_edges(s)
        if s == 2:
            for kh in range(3):
                weight_taps(1, kh)
            to_peer(1)
            for copy in peer_chunk(0):
                copy.wait_recv()
            gather(3)
        else:
            weight_taps(0, 2)
            to_peer(2)
            weight_taps(0, 1)
            to_peer(3)
            weight_taps(0, 0)
            to_peer(4)

    for copy in peer_chunk(1):
        copy.wait_recv()
    gather(2)
    for copy in peer_chunk(2):
        copy.wait_recv()
    gather(1)
    for chunk in (3, 4):
        for copy in peer_chunk(chunk):
            copy.wait_recv()
    gather(0)
    for kw in range(3):
        total = None
        for kt in range(3):
            for kh in range(3):
                more = jnp.dot(
                    cells_of(kt, kh, kw), w_v[9 * kt + 3 * kh + kw], preferred_element_type=F32
                )
                total = more if total is None else total + more
        part[kw] = total

    act_grad = part[1] + roll_w(part[2], True) + roll_w(part[0], False)
    feat = f_v[...].reshape(512, C).astype(F32)
    scale = lax.rsqrt(jnp.mean(feat * feat, axis=-1, keepdims=True) + EPS)
    unit = feat * scale
    normed = unit * gain
    sig = jax.nn.sigmoid(normed)
    normed_grad = act_grad * (sig * (1.0 + normed * (1.0 - sig)))
    gain_local = jnp.sum(normed_grad * unit, axis=0, keepdims=True)
    unit_grad = normed_grad * gain
    lean = jnp.mean(unit_grad * unit, axis=-1, keepdims=True)
    feat_grad = scale * (unit_grad - unit * lean)
    grad = gx[1, pl.ds(0, 2), pl.ds(1, 16)].reshape(512, C).astype(F32)
    ig[...] = (grad + feat_grad).astype(BF16).reshape(2, 16, 16, C)

    tokens = []
    for d in range(1, 16):
        there = lax.rem(col + d, 16)
        tokens.append(
            remote(
                ig.at[:, there],
                ig_out.at[:, pl.ds(pl.multiple_of(16 * col, 16), 16)],
                a_ss.at[d - 1],
                a_rs.at[d - 1],
                moved(col=d),
            )
        )
    for copy in tokens:
        copy.start()
    ig_out[:, pl.ds(pl.multiple_of(16 * col, 16), 16)] = ig[:, col]

    gs[0] = jnp.zeros((8, 128), F32)
    gs[0, pl.ds(0, 1), :] = gain_local[:, :128]
    gs[0, pl.ds(1, 1), pl.ds(0, 64)] = gain_local[:, 128:]
    gain_copies = []

    def gain_send(stage, slot, where):
        copy = remote(gs.at[stage], gr.at[slot], g_ss.at[slot], g_rs.at[slot], where)
        copy.start()
        gain_copies.append(copy)

    def gain_sum(stage, slots):
        total = gs[stage]
        for slot in slots:
            gain_copies[slot].wait_recv()
            total = total + gr[slot]
        return total

    gain_send(0, 0, peer)

    gs[1] = gain_sum(0, [0])
    for r in range(1, 4):
        gain_send(1, r, moved(row=r))

    second_rows(3)
    second_rows(2)
    gs[2] = gain_sum(1, [1, 2, 3])
    for t in range(1, 4):
        gain_send(2, 3 + t, moved(tm=-t))
    first_rows = [
        remote(p1a_s.at[r], p1a_r.at[r - 1], x_ss.at[r - 1], x_rs.at[r - 1], moved(row=r))
        for r in (1, 2, 3)
    ]
    for copy in first_rows:
        copy.wait_recv()
    t_a[...] = ffa[row] + p1a_r[0].astype(F32) + p1a_r[1].astype(F32) + p1a_r[2].astype(F32)
    for z in range(NA):
        a = t_a[81 * z : 81 * z + 48, :]
        b = t_a[81 * z + HALF : 81 * z + HALF + 48, :]
        top = t_a[LO + HALF * z : LO + HALF * z + 48, :]
        for y, piece in enumerate(slices(a, b, top, pltpu.roll(top, 64, 1))):
            va[y, HALF * z : HALF * z + 48, :] = piece
    second_copies = []
    for t in (2, 1, 3):
        y = lax.rem(tm + t, 4)
        p2a_s[y] = va[y, 0:A2].astype(BF16)
        copy = remote(
            p2a_s.at[y], p2a_r.at[t - 1], y2_ss.at[t - 1], y2_rs.at[t - 1], moved(tm=t)
        )
        copy.start()
        second_copies.append(copy)
    second_rows(1)
    second_rows(0)
    def depth(z, whole, at):
        p3s[z] = whole[HALF * at : HALF * at + 48]
        d = lax.rem(z + 8 - zed, 8)

        @pl.when(d != 0)
        def _():
            remote(
                p3s.at[z], p3r.at[d - 1], z_ss.at[d - 1], z_rs.at[d - 1],
                (tm, row, 2 * z + core),
            ).start()

    def a_part():
        for copy in second_copies:
            copy.wait_recv()
        u_a[0:A2] = (
            va[tm, 0:A2] + p2a_r[0].astype(F32) + p2a_r[1].astype(F32) + p2a_r[2].astype(F32)
        )
        for i, z in enumerate(ZA):
            depth(z, u_a, i)

    across = [
        remote(p2b_s.at[r], p2b_r.at[r - 1], x2_ss.at[r - 1], x2_rs.at[r - 1], moved(row=r))
        for r in (1, 2, 3)
    ]

    def b_part():
        for copy in across:
            copy.wait_recv()
        u_b[0:B1] = (
            t_b[row] + p2b_r[0].astype(F32) + p2b_r[1].astype(F32) + p2b_r[2].astype(F32)
        )
        for i, z in enumerate(ZB):
            depth(z, u_b, i)

    a_part()
    gs[3] = gain_sum(2, [4, 5, 6])
    for d in range(1, 8):
        gain_send(3, 6 + d, moved(col=2 * d))
    b_part()
    depth_copies = [
        remote(p3s.at[d], p3r.at[d - 1], z_ss.at[d - 1], z_rs.at[d - 1], moved(col=2 * d))
        for d in range(1, 8)
    ]
    total = p3s[zed]
    for d in range(7):
        depth_copies[d].wait_recv()
        total = total + p3r[d]
    wg_out[...] = total
    gg_out[...] = gain_sum(3, [7, 8, 9, 10, 11, 12, 13])

    for copy in tokens:
        copy.wait()
    for copy in halo + edges + first_rows + second_copies + across:
        copy.wait_send()
    for copy in depth_copies + gain_copies:
        copy.wait_send()
    for x in range(4):
        for t in range(1, 4):
            first_columns(x, t).wait_send()
    for chunk in range(len(PEER_CHUNKS)):
        for copy in peer_chunk(chunk):
            copy.wait_send()


def finish(ig_ref, wg_ref, gg_ref, ig_out, wg_out, gg_out):
    for f in range(2):
        wide = jnp.concatenate([ig_ref[f].astype(F32), jnp.zeros((256, 64), F32)], axis=1)
        ig_out[f] = jnp.transpose(wide)[:C].astype(BF16)
    square = jnp.concatenate([wg_ref[...], jnp.zeros((80, 128), F32)], axis=0)
    turned = jnp.transpose(square)
    wg_out[:, 0:41] = turned[0:48, 0:41]
    wg_out[:, 41:81] = turned[64:112, 0:40]
    gg_out[:, 0:128] = gg_ref[0:1]
    gg_out[:, 128:192] = gg_ref[1:2, 0:64]


def shards(features, norm_gain, conv_weight, out_grad):
    any_spec = pl.BlockSpec(memory_space=pl.ANY)
    vmem = pl.BlockSpec(memory_space=pltpu.VMEM)
    dma = pltpu.SemaphoreType.DMA
    scratch = [
        pltpu.VMEM((2, 16, 16, C), BF16),
        pltpu.VMEM((3, 4, 18, 16, C), BF16),
        pltpu.VMEM((C, 27 * C), BF16),
        pltpu.VMEM((27, C, C), BF16),
        pltpu.VMEM((2, 48, C), BF16),
        pltpu.VMEM((2, 2, 48, C), BF16),
        pltpu.VMEM((2, 48, C), F32),
        pltpu.VMEM((3, C, 512), BF16),
        pltpu.VMEM((3, 512, C), F32),
        pltpu.VMEM((5192, 128), F32),
        pltpu.VMEM((5192, 128), F32),
        pltpu.VMEM((5192, 128), F32),
        pltpu.VMEM((5192, 128), F32),
        pltpu.VMEM((4, A1, 128), F32),
        pltpu.VMEM((4, A1, 128), BF16),
        pltpu.VMEM((3, A1, 128), BF16),
        pltpu.VMEM((A1, 128), F32),
        pltpu.VMEM((4, 4, B1_SCRATCH, 128), F32),
        pltpu.VMEM((4, 4, B1, 128), BF16),
        pltpu.VMEM((3, 4, B1, 128), BF16),
        pltpu.VMEM((4, B1, 128), F32),
        pltpu.VMEM((4, A2_SCRATCH, 128), F32),
        pltpu.VMEM((4, A2, 128), BF16),
        pltpu.VMEM((3, A2, 128), BF16),
        pltpu.VMEM((A2_SCRATCH, 128), F32),
        pltpu.VMEM((4, B1, 128), BF16),
        pltpu.VMEM((3, B1, 128), BF16),
        pltpu.VMEM((B1_SCRATCH, 128), F32),
        pltpu.VMEM((8, 48, 128), F32),
        pltpu.VMEM((7, 48, 128), F32),
        pltpu.VMEM((4, 8, 128), F32),
        pltpu.VMEM((14, 8, 128), F32),
        pltpu.VMEM((2, 16, 16, C), BF16),
        dma((3,)),
        dma((6,)), dma((6,)),
        dma((4,)), dma((4,)),
        dma((10,)), dma((10,)),
        dma((3,)), dma((3,)),
        dma((12,)), dma((12,)),
        dma((3,)), dma((3,)),
        dma((3,)), dma((3,)),
        dma((7,)), dma((7,)),
        dma((15,)), dma((15,)),
        dma((14,)), dma((14,)),
    ]
    ig, wg, gg = pl.pallas_call(
        kernel,
        out_shape=(
            jax.ShapeDtypeStruct((2, 256, C), BF16),
            jax.ShapeDtypeStruct((48, 128), F32),
            jax.ShapeDtypeStruct((8, 128), F32),
        ),
        in_specs=[any_spec, vmem, any_spec, any_spec],
        out_specs=(vmem, vmem, vmem),
        scratch_shapes=scratch,
        compiler_params=pltpu.CompilerParams(
            collective_id=0, has_side_effects=True, vmem_limit_bytes=56 * 2**20
        ),
        name="unit_backward",
    )(features, norm_gain.reshape(1, C), conv_weight.T, out_grad)
    ig, wg, gg = pl.pallas_call(
        finish,
        out_shape=(
            jax.ShapeDtypeStruct((2, C, 256), BF16),
            jax.ShapeDtypeStruct((48, 81), F32),
            jax.ShapeDtypeStruct((1, C), F32),
        ),
        in_specs=[vmem, vmem, vmem],
        out_specs=(vmem, vmem, vmem),
        name="finish",
    )(ig, wg, gg)
    return ig.transpose(0, 2, 1)[:, None], wg.T, gg.reshape(C)


def solution(mesh):
    in_specs = (P("tm", "row", "col", None), P(), P(), P("tm", "row", "col", None))
    out_specs = (P("tm", ("row", "col"), None, None), P(("row", "col"), "tm"), P())
    return jax.shard_map(shards, mesh=mesh, in_specs=in_specs, out_specs=out_specs, check_vma=False)
```
